32 devices in a mesh: groups: 2 (over x), pair: 16 (over z, y, core).
Axes of the slice: x: 2, y: 2, z: 4, core: 2. Of those that a mesh axis runs over, the one named last changes fastest.
Arguments:
- right_side: float32 [512, 4096], P(('groups', 'pair')), parts along dimension 0, may hold values from -6 to 6
- pno_energy: float32 [512, 64], P(('groups', 'pair')), parts along dimension 0, may hold values from 1 to 4
- occ_energy: float32 [512], P(('groups', 'pair')), parts along dimension 0, may hold values from -2 to -0.5
- pno_count: int32 [512], P(('groups', 'pair')), parts along dimension 0, may hold values from 32 to 64
- margins: bfloat16 [512, 40, 4096], P(('groups', 'pair')), parts along dimension 0, may hold values from -0.4375 to 0.4375
- partners: int32 [512, 40], P(('groups', 'pair')), parts along dimension 0, may hold values from 0 to 255, as said below
- slot_of: int32 [512], P('groups'), parts along dimension 0, may hold values from 0 to 255, as said below
Outputs:
- solution: float32 [512, 4096], P(('groups', 'pair')), parts along dimension 0
- residual: float32 [512, 4096], P(('groups', 'pair')), parts along dimension 0
The draws below stay inside these ranges and needn't reach their ends.
There are 2 independent parts, one for each index of `groups`. The reference program is written for one: setup_inputs(seed, part) draws one part's arguments, and reference() takes and returns one part's arrays. A program takes and returns all parts, laid end to end along the dimension named above; each array names one. Nothing has to cross between parts.
Inputs may be any that keep to these rules, and one draw needn't show every extreme that they name: slot_of is a permutation of the pair ids; slot s is held by device s // 16 of the pair axis. `partners`: over the rows of one device, at most 54 entries name pairs stored on one device, and in every draw each device has some storing device that it names exactly 54 times.
All inputs are finite; a program needn't handle non-finite values.
Results may differ from the reference program's by a relative error of at most 0.0017.
The reference program's roundings to bfloat16 on the way (of `blocks` and `half`) count: a program that leaves them out, or rounds other values in their place, can miss the bound.
Values may be sent and summed in bfloat16 or wider, within the bound.
No kernel may reach another device: no remote copies, remote signals or barrier semaphores. Data moves between devices by JAX's collectives and lax.ppermute only.
A program may use at most 192 MiB of HBM per device.

```python
import jax
import jax.numpy as jnp
from jax import lax

NPNO = 64
COUPLE = 40
ITERS = 2
PAIRS_DEV = 16
PAIRS = 256
SENDS = 640
CAP = 54
N_PAIR = 16


def storage_order(key):
    return jax.random.permutation(jax.random.fold_in(key, 11), PAIRS).astype(jnp.int32)


def draw_slot_of(key, part):
    order = storage_order(key)
    return order


def draw_partners(key, part):
    order = storage_order(key)
    inverse = jnp.argsort(order).astype(jnp.int32)
    key = jax.random.fold_in(key, 5)
    devices = PAIRS // PAIRS_DEV
    slots = devices * CAP
    slot_device = (jnp.arange(slots) // CAP).astype(jnp.int32)

    def one_device(device_key):
        first, second, third, fourth = jax.random.split(device_key, 4)
        fullest = jax.random.randint(first, (), 0, devices)
        shuffle = jax.random.permutation(second, slots).astype(jnp.int32)
        score = jnp.where(slot_device == fullest, shuffle - slots, shuffle)
        chosen = jnp.argsort(score)[:SENDS]
        holders = slot_device[chosen]
        holders = holders[jax.random.permutation(third, SENDS)]
        within = jax.random.randint(fourth, (SENDS,), 0, PAIRS_DEV)
        return (holders * PAIRS_DEV + within).astype(jnp.int32)
    targets = jax.vmap(one_device)(jax.random.split(key, devices)).reshape(PAIRS, COUPLE)
    return inverse[targets].astype(jnp.int32)


def touch_ends(values, own_key, least, largest):
    longest = values.shape.index(max(values.shape))
    spots = []
    for shift in (0, 1):
        where = [jax.random.randint(jax.random.fold_in(own_key, axis), (), 0, length) for axis, length in enumerate(values.shape)]
        where[longest] = (where[longest] + shift) % values.shape[longest]
        spots.append(tuple(where))
    return values.at[spots[0]].set(least).at[spots[1]].set(largest)


def levels(stream_key, extent, cuts, smallest, largest):
    def one(position, blocks):
        steps = jax.random.uniform(jax.random.fold_in(jax.random.fold_in(stream_key, 6), position), (blocks,), jnp.float32, smallest / len(cuts), largest / len(cuts))
        return jnp.repeat(jnp.exp(steps), extent[position] // blocks).reshape((-1,) + (1,) * (len(extent) - position - 1))

    loudness = one(*cuts[0])
    for cut in cuts[1:]:
        loudness = loudness * one(*cut)
    return loudness


def noise(stream_key, extent, spread, most, pieces=(), dtype=jnp.bfloat16):
    entries = jax.random.normal(stream_key, extent, jnp.float32) * spread
    if len(pieces) > 0:
        entries = levels(stream_key, extent, pieces, -0.22, 0.18) * entries
    return jnp.clip(entries, min=-most, max=most).astype(dtype)


def setup_inputs(seed: int = 0, part: int = 0) -> dict:
    key_list = jax.random.split(jax.random.key(seed), 8)
    part_keys = jax.random.split(jax.random.fold_in(key_list[7], part), 8)
    right_side = noise(part_keys[0], (PAIRS, NPNO * NPNO), 1.0, 6.0, ((0, 16),), jnp.float32)
    pno_energy = jnp.clip(1.0 + 3.0 * jax.random.uniform(part_keys[1], (PAIRS, NPNO), jnp.float32) ** levels(part_keys[1], (PAIRS, NPNO), ((0, 16),), -0.2, 0.2), 1.0, 4.0)
    occ_energy = jnp.clip(-2.0 + 1.5 * jax.random.uniform(part_keys[2], (PAIRS,), jnp.float32) ** levels(part_keys[2], (PAIRS,), ((0, 16),), -0.2, 0.2), -2.0, -0.5)
    pno_count = touch_ends(jax.random.randint(part_keys[3], (PAIRS,), NPNO // 2, NPNO + 1), jax.random.fold_in(part_keys[3], 1), NPNO // 2, NPNO).astype(jnp.int32)
    margins = noise(part_keys[4], (PAIRS, COUPLE, NPNO * NPNO), (3 * NPNO) ** -0.5, 0.4375, ((0, 16),))
    partners = draw_partners(jax.random.fold_in(jax.random.fold_in(key_list[7], part), 71), part)
    slot_of = draw_slot_of(jax.random.fold_in(jax.random.fold_in(key_list[7], part), 71), part)
    return {"right_side": right_side, "pno_energy": pno_energy, "occ_energy": occ_energy, "pno_count": pno_count, "margins": margins, "partners": partners, "slot_of": slot_of}


FREQUENCY = 0.25


def reference(right_side, pno_energy, occ_energy, pno_count, margins, partners, slot_of):
    count_mask = (jnp.arange(NPNO)[None, :] < pno_count[:, None]).astype(jnp.float32)
    mask = (count_mask[:, :, None] * count_mask[:, None, :]).reshape(PAIRS, NPNO * NPNO)
    denom = (pno_energy[:, :, None] + pno_energy[:, None, :]).reshape(PAIRS, NPNO * NPNO)
    denom = denom - occ_energy[:, None] - FREQUENCY
    solution = mask * right_side / denom
    target = slot_of[partners].astype(jnp.int32)
    margin_blocks = margins.reshape(N_PAIR, PAIRS_DEV, COUPLE, NPNO, NPNO)
    target_blocks = target.reshape(N_PAIR, PAIRS_DEV, COUPLE)
    residual = jnp.zeros_like(solution)
    for step in range(ITERS):
        blocks = solution.astype(jnp.bfloat16)

        def couple(operands):
            margin_block, target_block = operands
            fetched = blocks[target_block].reshape(PAIRS_DEV, COUPLE, NPNO, NPNO).astype(jnp.float32)
            wide_margin = margin_block.astype(jnp.float32)
            half = jnp.einsum('pkab,pkbc->pkac', wide_margin, fetched).astype(jnp.bfloat16)
            half = lax.optimization_barrier(half).astype(jnp.float32)
            return jnp.einsum('pkac,pkdc->pad', half, wide_margin).reshape(PAIRS_DEV, NPNO * NPNO)

        coupled = lax.map(couple, (margin_blocks, target_blocks)).reshape(PAIRS, NPNO * NPNO)
        residual = mask * (right_side - denom * solution - coupled)
        solution = solution + residual / denom
    return solution, residual
```

```python
import functools

import jax
import jax.numpy as jnp
from jax import lax
from jax.experimental import pallas as pl
from jax.experimental.pallas import tpu as pltpu
from jax.sharding import PartitionSpec as P

ITERS = 2
FREQUENCY = 0.25
SLOTS_AT_ONCE = 4
NT = (((1,), (1,)), ((), ()))
VMEM = pl.BlockSpec(memory_space=pltpu.VMEM)
SMEM = pl.BlockSpec(memory_space=pltpu.SMEM)
ANY = pl.BlockSpec(memory_space=pl.ANY)


def left_lanes(width):
    return lax.broadcasted_iota(jnp.int32, (width, 2 * width), 1) < width


def swap_halves(tile):
    width = tile.shape[1] // 2
    return jnp.concatenate([tile[:, width:], tile[:, :width]], axis=1)


def start_kernel(count, occ, right, energy, right_out, denom_out, mask_out, solution_out, blocks_out, rows):
    slots, width = energy.shape
    half = slots // 2
    lanes = 2 * width
    slot = lax.broadcasted_iota(jnp.int32, (slots, lanes), 0)
    for j in range(width // 2):
        part = right[:, j * lanes : (j + 1) * lanes]
        turned = swap_halves(part)
        rows[pl.ds(2 * j, slots, stride=width), :] = jnp.where(slot < half, part, turned)
        rows[pl.ds(2 * j + 1, slots, stride=width), :] = jnp.where(slot < half, turned, part)
    left = left_lanes(width)
    row = lax.broadcasted_iota(jnp.int32, (width, lanes), 0)
    column = lax.broadcasted_iota(jnp.int32, (width, lanes), 1) % width
    across = energy[...]
    down = across.T
    for u in range(half):
        v = u + half
        first = jnp.broadcast_to(down[:, u : u + 1], (width, lanes))
        second = jnp.broadcast_to(down[:, v : v + 1], (width, lanes))
        along = jnp.concatenate([across[u : u + 1], across[v : v + 1]], axis=1)
        shift = jnp.where(left, occ[u], occ[v])
        denom = jnp.where(left, first, second) + along - shift - FREQUENCY
        most = jnp.where(left, count[u], count[v])
        mask = jnp.where((row < most) & (column < most), 1.0, 0.0)
        tile = jnp.where(left, rows[u * width : (u + 1) * width], rows[v * width : (v + 1) * width])
        now = mask * tile / denom
        right_out[u] = tile
        denom_out[u] = denom
        mask_out[u] = mask
        solution_out[u] = now
        blocks_out[u] = now.astype(jnp.bfloat16)


def start(right_side, pno_energy, occ_energy, pno_count):
    slots, width = pno_energy.shape
    tiles = jax.ShapeDtypeStruct((slots // 2, width, 2 * width), jnp.float32)
    return pl.pallas_call(
        start_kernel,
        in_specs=[SMEM, SMEM, VMEM, VMEM],
        out_specs=[VMEM] * 5,
        out_shape=[tiles] * 4 + [jax.ShapeDtypeStruct(tiles.shape, jnp.bfloat16)],
        scratch_shapes=[pltpu.VMEM((slots * width, 2 * width), jnp.float32)],
        name="start",
    )(pno_count, occ_energy, right_side, pno_energy)


def margin_kernel(margins, tiles, rows):
    partners = margins.shape[1]
    width = tiles.shape[2]
    lanes = 2 * width
    even = lax.broadcasted_iota(jnp.int32, (partners, lanes), 0) % 2 == 0
    for j in range(width // 2):
        part = margins[0, :, j * lanes : (j + 1) * lanes].astype(jnp.float32)
        turned = swap_halves(part)
        rows[pl.ds(2 * j, partners, stride=width), :] = jnp.where(even, part, turned)
        rows[pl.ds(2 * j + 1, partners, stride=width), :] = jnp.where(even, turned, part)
    left = left_lanes(width)
    for k in range(partners // 2):
        first = rows[2 * k * width : (2 * k + 1) * width]
        second = rows[(2 * k + 1) * width : (2 * k + 2) * width]
        tiles[0, k] = jnp.where(left, first, second).astype(jnp.bfloat16)


def margin_tiles(margins, width):
    slots, partners, flat = margins.shape
    return pl.pallas_call(
        margin_kernel,
        grid=(slots,),
        in_specs=[pl.BlockSpec((1, partners, flat), lambda s: (s, 0, 0))],
        out_specs=pl.BlockSpec((1, partners // 2, width, 2 * width), lambda s: (s, 0, 0, 0)),
        out_shape=jax.ShapeDtypeStruct((slots, partners // 2, width, 2 * width), jnp.bfloat16),
        scratch_shapes=[pltpu.VMEM((partners * width, 2 * width), jnp.float32)],
        cost_estimate=pl.CostEstimate(flops=0, bytes_accessed=16 * margins.size, transcendentals=0),
        name="margin_tiles",
    )(margins)


def couple_kernel(last, pieces, twist, partners, slot_of, *refs):
    gathered, refs = refs[:pieces], refs[pieces:]
    margins, right, denom, mask, current, solution_out, residual_out = refs[:7]
    blocks_out, refs = (None, refs[7:]) if last else (refs[7], refs[8:])
    expanded, held, halves, coupled, arrived = refs[:5]
    slots, pairs, width, lanes = margins.shape
    half = slots // 2
    count = 2 * pairs

    def fetch(s):
        return pltpu.make_async_copy(margins.at[s], held.at[s], arrived.at[s])

    for s in range(slots):
        fetch(s).start()

    left = left_lanes(width)
    base = 0
    for piece in gathered:
        held_devices = piece.shape[0] // half

        def expand(i, carry, piece=piece, base=base):
            tile = piece[i]
            turned = swap_halves(tile)
            zero = jnp.zeros_like(tile)
            u = (base + i // half) * slots + i % half
            v = u + half
            expanded[2 * u] = jnp.where(left, tile, zero)
            expanded[2 * u + 1] = jnp.where(left, zero, turned)
            expanded[2 * v] = jnp.where(left, turned, zero)
            expanded[2 * v + 1] = jnp.where(left, zero, tile)
            return carry

        lax.fori_loop(0, piece.shape[0], expand, 0, unroll=4)
        base += held_devices

    turn = twist[0] * slots

    def block(s, k):
        target = slot_of[partners[s, k]] ^ turn
        return expanded[2 * target + k % 2]

    zero = jnp.zeros((lanes, lanes), jnp.bfloat16)

    def one_slot(s, at):
        for q in range(pairs // 2):
            upper = jnp.concatenate([block(s, 4 * q), block(s, 4 * q + 1)], axis=0)
            lower = jnp.concatenate([block(s, 4 * q + 2), block(s, 4 * q + 3)], axis=0)
            weights = jnp.concatenate(
                [jnp.concatenate([upper, zero], axis=1), jnp.concatenate([zero, lower], axis=1)], axis=0
            )
            margin = jnp.concatenate([held[s, 2 * q], held[s, 2 * q + 1]], axis=1)
            product = jnp.dot(margin, weights, preferred_element_type=jnp.float32)
            halves[at, :, 2 * q * lanes : 2 * (q + 1) * lanes] = product.astype(jnp.bfloat16)
        margin = jnp.concatenate([held[s, k] for k in range(pairs)], axis=1)
        coupled[s] = lax.dot_general(halves[at], margin, NT, preferred_element_type=jnp.float32)

    def some_slots(i, carry):
        for at in range(SLOTS_AT_ONCE):
            fetch(i * SLOTS_AT_ONCE + at).wait()
        for at in range(SLOTS_AT_ONCE):
            one_slot(i * SLOTS_AT_ONCE + at, at)
        return carry

    lax.fori_loop(0, slots // SLOTS_AT_ONCE, some_slots, 0)

    if last:
        store = refs[5]
    for u in range(half):
        both = jnp.concatenate([coupled[u], coupled[u + half]], axis=1)
        before = current[u]
        residual = mask[u] * (right[u] - denom[u] * before - both)
        after = before + residual / denom[u]
        if last:
            for n, tile in enumerate((after, residual)):
                store[2 * n, u * width : (u + 1) * width] = tile
                store[2 * n + 1, u * width : (u + 1) * width] = swap_halves(tile)
        else:
            solution_out[u] = after
            residual_out[u] = residual
            blocks_out[u] = after.astype(jnp.bfloat16)
    if last:
        keep = lax.broadcasted_iota(jnp.int32, (half, lanes), 1) < width
        for n, out in enumerate((solution_out, residual_out)):
            for j in range(width // 2):
                upper = store[2 * n, pl.ds(2 * j, half, stride=width), :]
                lower = store[2 * n, pl.ds(2 * j + 1, half, stride=width), :]
                upper_turned = store[2 * n + 1, pl.ds(2 * j, half, stride=width), :]
                lower_turned = store[2 * n + 1, pl.ds(2 * j + 1, half, stride=width), :]
                out[:half, j * lanes : (j + 1) * lanes] = jnp.where(keep, upper, lower_turned)
                out[half:, j * lanes : (j + 1) * lanes] = jnp.where(keep, upper_turned, lower)


def couple(last, twist, partners, slot_of, gathered, margins, right, denom, mask, current):
    slots, pairs, width, lanes = margins.shape
    half = slots // 2
    devices = sum(piece.shape[0] for piece in gathered) // half
    packed = jax.ShapeDtypeStruct((half, width, lanes), jnp.float32)
    flat = jax.ShapeDtypeStruct((slots, width * width), jnp.float32)
    blocks = jax.ShapeDtypeStruct((half, width, lanes), jnp.bfloat16)
    outs = [flat, flat] if last else [packed, packed, blocks]
    scratch = [
        pltpu.VMEM((2 * devices * slots, width, lanes), jnp.bfloat16),
        pltpu.VMEM(margins.shape, jnp.bfloat16),
        pltpu.VMEM((SLOTS_AT_ONCE, width, pairs * lanes), jnp.bfloat16),
        pltpu.VMEM((slots, width, width), jnp.float32),
        pltpu.SemaphoreType.DMA((slots,)),
    ]
    if last:
        scratch.append(pltpu.VMEM((4, half * width, lanes), jnp.float32))
    return pl.pallas_call(
        functools.partial(couple_kernel, last, len(gathered)),
        in_specs=[SMEM] * 3 + [VMEM] * len(gathered) + [ANY] + [VMEM] * 4,
        out_specs=[VMEM] * len(outs),
        out_shape=outs,
        scratch_shapes=scratch,
        compiler_params=pltpu.CompilerParams(vmem_limit_bytes=56 * 2**20),
        name="couple",
    )(twist, partners, slot_of, *gathered, margins, right, denom, mask, current)


def gather(blocks, devices):
    if devices != 16:
        return [lax.all_gather(blocks, "pair", axis=0, tiled=True)], jnp.zeros((1,), jnp.int32)

    def swap(piece, other):
        return lax.ppermute(piece, "pair", [(i, i ^ other) for i in range(devices)])

    piece = {0: blocks}
    for other in (2, 4, 12):
        piece[other] = swap(blocks, other)
    piece[8] = swap(piece[12], 4)
    for other in (4, 12, 8):
        piece[other ^ 2] = swap(piece[other], 2)
    for other in (0, 2, 4, 6, 12, 14, 8, 10):
        piece[other ^ 1] = swap(piece[other], 1)
    return [piece[i] for i in range(devices)], lax.axis_index("pair").astype(jnp.int32).reshape(1)


def shards(right_side, pno_energy, occ_energy, pno_count, margins, partners, slot_of):
    devices = lax.axis_size("pair")
    right, denom, mask, current, blocks = start(right_side, pno_energy, occ_energy, pno_count)
    tiles = margin_tiles(margins, pno_energy.shape[1])
    for step in range(ITERS):
        gathered, twist = gather(blocks, devices)
        outs = couple(step == ITERS - 1, twist, partners, slot_of, gathered, tiles, right, denom, mask, current)
        if step < ITERS - 1:
            current, _, blocks = outs
    return tuple(outs)


def solution(mesh):
    placed = (
        P(("groups", "pair"), None),
        P(("groups", "pair"), None),
        P(("groups", "pair")),
        P(("groups", "pair")),
        P(("groups", "pair"), None, None),
        P(("groups", "pair"), None),
        P("groups"),
    )
    return jax.shard_map(
        shards,
        mesh=mesh,
        in_specs=placed,
        out_specs=(P(("groups", "pair"), None), P(("groups", "pair"), None)),
        check_vma=False,
    )
```

```python
import functools
import math

import jax
import jax.numpy as jnp
import numpy as np
from jax import lax
from jax.experimental import pallas as pl
from jax.experimental.pallas import tpu as pltpu
from jax.sharding import PartitionSpec as P

ITERS = 2
FREQUENCY = 0.25
SLOTS_AT_ONCE = 4
ENTRIES = 16
TILES = 8
PARTS = 4
NT = (((1,), (1,)), ((), ()))
VMEM = pl.BlockSpec(memory_space=pltpu.VMEM)
SMEM = pl.BlockSpec(memory_space=pltpu.SMEM)
ANY = pl.BlockSpec(memory_space=pl.ANY)


def left_lanes(width):
    return lax.broadcasted_iota(jnp.int32, (width, 2 * width), 1) < width


def swap_halves(tile):
    width = tile.shape[1] // 2
    return jnp.concatenate([tile[:, width:], tile[:, :width]], axis=1)


def start_kernel(count, occ, right, energy, right_out, denom_out, mask_out, solution_out, blocks_out, rows):
    slots, width = energy.shape
    half = slots // 2
    lanes = 2 * width
    slot = lax.broadcasted_iota(jnp.int32, (slots, lanes), 0)
    for j in range(width // 2):
        part = right[:, j * lanes : (j + 1) * lanes]
        turned = swap_halves(part)
        rows[pl.ds(2 * j, slots, stride=width), :] = jnp.where(slot < half, part, turned)
        rows[pl.ds(2 * j + 1, slots, stride=width), :] = jnp.where(slot < half, turned, part)
    left = left_lanes(width)
    row = lax.broadcasted_iota(jnp.int32, (width, lanes), 0)
    column = lax.broadcasted_iota(jnp.int32, (width, lanes), 1) % width
    across = energy[...]
    down = across.T
    for u in range(half):
        v = u + half
        first = jnp.broadcast_to(down[:, u : u + 1], (width, lanes))
        second = jnp.broadcast_to(down[:, v : v + 1], (width, lanes))
        along = jnp.concatenate([across[u : u + 1], across[v : v + 1]], axis=1)
        shift = jnp.where(left, occ[u], occ[v])
        denom = jnp.where(left, first, second) + along - shift - FREQUENCY
        most = jnp.where(left, count[u], count[v])
        mask = jnp.where((row < most) & (column < most), 1.0, 0.0)
        tile = jnp.where(left, rows[u * width : (u + 1) * width], rows[v * width : (v + 1) * width])
        now = mask * tile / denom
        right_out[u] = tile
        denom_out[u] = denom
        mask_out[u] = mask
        solution_out[u] = now
        blocks_out[u] = now.astype(jnp.bfloat16)


def start(right_side, pno_energy, occ_energy, pno_count):
    slots, width = pno_energy.shape
    tiles = jax.ShapeDtypeStruct((slots // 2, width, 2 * width), jnp.float32)
    return pl.pallas_call(
        start_kernel,
        in_specs=[SMEM, SMEM, VMEM, VMEM],
        out_specs=[VMEM] * 5,
        out_shape=[tiles] * 4 + [jax.ShapeDtypeStruct(tiles.shape, jnp.bfloat16)],
        scratch_shapes=[pltpu.VMEM((slots * width, 2 * width), jnp.float32)],
        name="start",
    )(pno_count, occ_energy, right_side, pno_energy)


def picker():
    pair, line = np.divmod(np.arange(ENTRIES * TILES), 2 * TILES)
    ones = np.zeros((ENTRIES * TILES, 2 * TILES * ENTRIES), np.float32)
    for side in range(2):
        ones[np.arange(ENTRIES * TILES), (line % 2) * TILES * ENTRIES + (line // 2) * ENTRIES + 2 * pair + side] = 1
    return jnp.asarray(ones, jnp.bfloat16)


def margin_kernel(pick, margins, tiles):
    width, lanes = tiles.shape[1:]
    left = lax.broadcasted_iota(jnp.int32, (ENTRIES, lanes), 1) < width
    even = lax.broadcasted_iota(jnp.int32, (ENTRIES, lanes), 0) % 2 == 0
    ones = pick[...]
    for group in range(margins.shape[0] // ENTRIES):
        rows = slice(group * ENTRIES, (group + 1) * ENTRIES)
        for n in range(0, width // 2, 2 * TILES):
            sides = []
            for part in (n, n + TILES):
                upper, lower = [], []
                for j in range(part, part + TILES):
                    here = margins[rows, j * lanes : (j + 1) * lanes]
                    turned = swap_halves(here)
                    zero = jnp.zeros_like(here)
                    upper.append(jnp.where(left & even, here, jnp.where(left | even, zero, turned)))
                    lower.append(jnp.where(left & even, turned, jnp.where(left | even, zero, here)))
                sides.append(jnp.concatenate(upper + lower, axis=0))
            both = jnp.concatenate(sides, axis=1)
            found = jnp.dot(ones, both, preferred_element_type=jnp.float32).astype(jnp.bfloat16)
            for pair in range(ENTRIES // 2):
                for side in range(2):
                    line = 2 * (n + side * TILES)
                    tiles[group * ENTRIES // 2 + pair, line : line + 2 * TILES] = found[
                        pair * 2 * TILES : (pair + 1) * 2 * TILES, side * lanes : (side + 1) * lanes
                    ]


def margin_tiles(margins, width):
    slots, partners, flat = margins.shape
    rows = margins.reshape(slots * partners, flat)
    step = ENTRIES * math.lcm(partners, ENTRIES) // ENTRIES
    part = slots * partners // PARTS
    pick = picker()
    parts = []
    for n in range(PARTS):
        tiles = pl.pallas_call(
            margin_kernel,
            grid=(part // step,),
            in_specs=[
                pl.BlockSpec(pick.shape, lambda i: (0, 0)),
                pl.BlockSpec((step, flat), lambda i, n=n: (n * (part // step) + i, 0)),
            ],
            out_specs=pl.BlockSpec((step // 2, width, 2 * width), lambda i: (i, 0, 0)),
            out_shape=jax.ShapeDtypeStruct((part // 2, width, 2 * width), jnp.bfloat16),
            cost_estimate=pl.CostEstimate(flops=0, bytes_accessed=4 * part * flat, transcendentals=0),
            compiler_params=pltpu.CompilerParams(vmem_limit_bytes=16 * 2**20),
            name="margin_tiles",
        )(pick, rows)
        parts.append(tiles.reshape(slots // PARTS, partners // 2, width, 2 * width))
    return parts


def couple_kernel(last, pieces, twist, partners, slot_of, *refs):
    gathered, refs = refs[:pieces], refs[pieces:]
    margins, refs = refs[:PARTS], refs[PARTS:]
    right, denom, mask, current = refs[:4]
    outs, refs = refs[4:6], refs[6:]
    expanded, held, halves, coupled, arrived = refs[:5]
    slots, pairs, width, lanes = held.shape
    half = slots // 2
    share = slots // PARTS

    def fetch(part):
        return pltpu.make_async_copy(margins[part], held.at[pl.ds(part * share, share)], arrived.at[part])

    for part in range(PARTS):
        fetch(part).start()

    left = left_lanes(width)
    base = 0
    for piece in gathered:
        held_devices = piece.shape[0] // half

        def expand(i, carry, piece=piece, base=base):
            tile = piece[i]
            turned = swap_halves(tile)
            zero = jnp.zeros_like(tile)
            u = (base + i // half) * slots + i % half
            v = u + half
            expanded[2 * u] = jnp.where(left, tile, zero)
            expanded[2 * u + 1] = jnp.where(left, zero, turned)
            expanded[2 * v] = jnp.where(left, turned, zero)
            expanded[2 * v + 1] = jnp.where(left, zero, tile)
            return carry

        lax.fori_loop(0, piece.shape[0], expand, 0, unroll=4)
        base += held_devices

    turn = twist[0] * slots

    def block(s, k):
        target = slot_of[partners[s, k]] ^ turn
        return expanded[2 * target + k % 2]

    zero = jnp.zeros((lanes, lanes), jnp.bfloat16)

    def one_slot(s, at):
        for q in range(pairs // 2):
            upper = jnp.concatenate([block(s, 4 * q), block(s, 4 * q + 1)], axis=0)
            lower = jnp.concatenate([block(s, 4 * q + 2), block(s, 4 * q + 3)], axis=0)
            weights = jnp.concatenate(
                [jnp.concatenate([upper, zero], axis=1), jnp.concatenate([zero, lower], axis=1)], axis=0
            )
            margin = jnp.concatenate([held[s, 2 * q], held[s, 2 * q + 1]], axis=1)
            product = jnp.dot(margin, weights, preferred_element_type=jnp.float32)
            halves[at, :, 2 * q * lanes : 2 * (q + 1) * lanes] = product.astype(jnp.bfloat16)
        margin = jnp.concatenate([held[s, k] for k in range(pairs)], axis=1)
        coupled[s] = lax.dot_general(halves[at], margin, NT, preferred_element_type=jnp.float32)

    def some_slots(i, carry):
        for at in range(SLOTS_AT_ONCE):
            one_slot(i * SLOTS_AT_ONCE + at, at)
        return carry

    for part in range(PARTS):
        fetch(part).wait()
    lax.fori_loop(0, slots // SLOTS_AT_ONCE, some_slots, 0)

    if last:
        store = refs[5]
    for u in range(half):
        both = jnp.concatenate([coupled[u], coupled[u + half]], axis=1)
        before = current[u]
        residual = mask[u] * (right[u] - denom[u] * before - both)
        after = before + residual / denom[u]
        if last:
            for n, tile in enumerate((after, residual)):
                store[2 * n, u * width : (u + 1) * width] = tile
                store[2 * n + 1, u * width : (u + 1) * width] = swap_halves(tile)
        else:
            outs[0][u] = after
            outs[1][u] = after.astype(jnp.bfloat16)
    if last:
        keep = lax.broadcasted_iota(jnp.int32, (half, lanes), 1) < width
        for n, out in enumerate(outs):
            for j in range(width // 2):
                upper = store[2 * n, pl.ds(2 * j, half, stride=width), :]
                lower = store[2 * n, pl.ds(2 * j + 1, half, stride=width), :]
                upper_turned = store[2 * n + 1, pl.ds(2 * j, half, stride=width), :]
                lower_turned = store[2 * n + 1, pl.ds(2 * j + 1, half, stride=width), :]
                out[:half, j * lanes : (j + 1) * lanes] = jnp.where(keep, upper, lower_turned)
                out[half:, j * lanes : (j + 1) * lanes] = jnp.where(keep, upper_turned, lower)


def couple(last, twist, partners, slot_of, gathered, margins, right, denom, mask, current):
    share, pairs, width, lanes = margins[0].shape
    slots = share * len(margins)
    half = slots // 2
    devices = sum(piece.shape[0] for piece in gathered) // half
    packed = jax.ShapeDtypeStruct((half, width, lanes), jnp.float32)
    flat = jax.ShapeDtypeStruct((slots, width * width), jnp.float32)
    blocks = jax.ShapeDtypeStruct((half, width, lanes), jnp.bfloat16)
    outs = [flat, flat] if last else [packed, blocks]
    scratch = [
        pltpu.VMEM((2 * devices * slots, width, lanes), jnp.bfloat16),
        pltpu.VMEM((slots, pairs, width, lanes), jnp.bfloat16),
        pltpu.VMEM((SLOTS_AT_ONCE, width, pairs * lanes), jnp.bfloat16),
        pltpu.VMEM((slots, width, width), jnp.float32),
        pltpu.SemaphoreType.DMA((len(margins),)),
    ]
    if last:
        scratch.append(pltpu.VMEM((4, half * width, lanes), jnp.float32))
    return pl.pallas_call(
        functools.partial(couple_kernel, last, len(gathered)),
        in_specs=[SMEM] * 3 + [VMEM] * len(gathered) + [ANY] * len(margins) + [VMEM] * 4,
        out_specs=[VMEM] * len(outs),
        out_shape=outs,
        scratch_shapes=scratch,
        compiler_params=pltpu.CompilerParams(vmem_limit_bytes=56 * 2**20),
        name="couple",
    )(twist, partners, slot_of, *gathered, *margins, right, denom, mask, current)


def gather(blocks, devices, meanwhile):
    if devices != 16:
        return [lax.all_gather(blocks, "pair", axis=0, tiled=True)], jnp.zeros((1,), jnp.int32)

    def swap(piece, other):
        return lax.ppermute(piece, "pair", [(i, i ^ other) for i in range(devices)])

    piece = {0: blocks}
    for other in (2, 4, 12):
        piece[other] = swap(blocks, other)
    piece[12], meanwhile[:2] = lax.optimization_barrier((piece[12], meanwhile[:2]))
    piece[8] = swap(piece[12], 4)
    piece[14] = swap(piece[12], 2)
    piece[10] = swap(piece[12], 6)
    piece[6] = swap(piece[4], 2)
    for other in (0, 2, 4, 12):
        piece[other ^ 1] = swap(piece[other], 1)
    for other in (6, 14, 8, 10):
        piece[other], meanwhile[2:] = lax.optimization_barrier((piece[other], meanwhile[2:]))
        piece[other ^ 1] = swap(piece[other], 1)
    return [piece[i] for i in range(devices)], lax.axis_index("pair").astype(jnp.int32).reshape(1)


def shards(right_side, pno_energy, occ_energy, pno_count, margins, partners, slot_of):
    devices = lax.axis_size("pair")
    right, denom, mask, current, blocks = start(right_side, pno_energy, occ_energy, pno_count)
    tiles = margin_tiles(margins, pno_energy.shape[1])
    for step in range(ITERS):
        gathered, twist = gather(blocks, devices, tiles if step == 0 else [])
        outs = couple(step == ITERS - 1, twist, partners, slot_of, gathered, tiles, right, denom, mask, current)
        if step < ITERS - 1:
            current, blocks = outs
    return tuple(outs)


def solution(mesh):
    placed = (
        P(("groups", "pair"), None),
        P(("groups", "pair"), None),
        P(("groups", "pair")),
        P(("groups", "pair")),
        P(("groups", "pair"), None, None),
        P(("groups", "pair"), None),
        P("groups"),
    )
    return jax.shard_map(
        shards,
        mesh=mesh,
        in_specs=placed,
        out_specs=(P(("groups", "pair"), None), P(("groups", "pair"), None)),
        check_vma=False,
    )
```

```python
import functools
import math

import jax
import jax.numpy as jnp
import numpy as np
from jax import lax
from jax.experimental import pallas as pl
from jax.experimental.pallas import tpu as pltpu
from jax.sharding import PartitionSpec as P

ITERS = 2
FREQUENCY = 0.25
SLOTS_AT_ONCE = 4
ENTRIES = 16
TILES = 8
NT = (((1,), (1,)), ((), ()))
VMEM = pl.BlockSpec(memory_space=pltpu.VMEM)
SMEM = pl.BlockSpec(memory_space=pltpu.SMEM)
ANY = pl.BlockSpec(memory_space=pl.ANY)


def left_lanes(width):
    return lax.broadcasted_iota(jnp.int32, (width, 2 * width), 1) < width


def swap_halves(tile):
    width = tile.shape[1] // 2
    return jnp.concatenate([tile[:, width:], tile[:, :width]], axis=1)


def start_kernel(count, occ, right, energy, right_out, denom_out, mask_out, solution_out, blocks_out, rows):
    slots, width = energy.shape
    half = slots // 2
    lanes = 2 * width
    slot = lax.broadcasted_iota(jnp.int32, (slots, lanes), 0)
    for j in range(width // 2):
        part = right[:, j * lanes : (j + 1) * lanes]
        turned = swap_halves(part)
        rows[pl.ds(2 * j, slots, stride=width), :] = jnp.where(slot < half, part, turned)
        rows[pl.ds(2 * j + 1, slots, stride=width), :] = jnp.where(slot < half, turned, part)
    left = left_lanes(width)
    row = lax.broadcasted_iota(jnp.int32, (width, lanes), 0)
    column = lax.broadcasted_iota(jnp.int32, (width, lanes), 1) % width
    across = energy[...]
    down = across.T
    for u in range(half):
        v = u + half
        first = jnp.broadcast_to(down[:, u : u + 1], (width, lanes))
        second = jnp.broadcast_to(down[:, v : v + 1], (width, lanes))
        along = jnp.concatenate([across[u : u + 1], across[v : v + 1]], axis=1)
        shift = jnp.where(left, occ[u], occ[v])
        denom = jnp.where(left, first, second) + along - shift - FREQUENCY
        most = jnp.where(left, count[u], count[v])
        mask = jnp.where((row < most) & (column < most), 1.0, 0.0)
        tile = jnp.where(left, rows[u * width : (u + 1) * width], rows[v * width : (v + 1) * width])
        now = mask * tile / denom
        right_out[u] = tile
        denom_out[u] = denom
        mask_out[u] = mask
        solution_out[u] = now
        blocks_out[u] = now.astype(jnp.bfloat16)


def start(right_side, pno_energy, occ_energy, pno_count):
    slots, width = pno_energy.shape
    tiles = jax.ShapeDtypeStruct((slots // 2, width, 2 * width), jnp.float32)
    return pl.pallas_call(
        start_kernel,
        in_specs=[SMEM, SMEM, VMEM, VMEM],
        out_specs=[VMEM] * 5,
        out_shape=[tiles] * 4 + [jax.ShapeDtypeStruct(tiles.shape, jnp.bfloat16)],
        scratch_shapes=[pltpu.VMEM((slots * width, 2 * width), jnp.float32)],
        name="start",
    )(pno_count, occ_energy, right_side, pno_energy)


def picker():
    pair, line = np.divmod(np.arange(ENTRIES * TILES), 2 * TILES)
    ones = np.zeros((ENTRIES * TILES, 2 * TILES * ENTRIES), np.float32)
    for side in range(2):
        ones[np.arange(ENTRIES * TILES), (line % 2) * TILES * ENTRIES + (line // 2) * ENTRIES + 2 * pair + side] = 1
    return jnp.asarray(ones, jnp.bfloat16)


def margin_kernel(pick, margins, tiles, held, arrived):
    width, lanes = tiles.shape[1:]
    steps, step = held.shape[:2]
    left = lax.broadcasted_iota(jnp.int32, (ENTRIES, lanes), 1) < width
    even = lax.broadcasted_iota(jnp.int32, (ENTRIES, lanes), 0) % 2 == 0

    def fetch(i):
        return pltpu.make_async_copy(margins.at[pl.ds(i * step, step)], held.at[i], arrived.at[i])

    for i in range(steps):
        fetch(i).start()
    ones = pick[...]

    def some(i, carry):
        fetch(i).wait()
        for group in range(step // ENTRIES):
            rows = slice(group * ENTRIES, (group + 1) * ENTRIES)
            for n in range(0, width // 2, 2 * TILES):
                sides = []
                for part in (n, n + TILES):
                    upper, lower = [], []
                    for j in range(part, part + TILES):
                        here = held[i, rows, j * lanes : (j + 1) * lanes]
                        turned = swap_halves(here)
                        zero = jnp.zeros_like(here)
                        upper.append(jnp.where(left & even, here, jnp.where(left | even, zero, turned)))
                        lower.append(jnp.where(left & even, turned, jnp.where(left | even, zero, here)))
                    sides.append(jnp.concatenate(upper + lower, axis=0))
                both = jnp.concatenate(sides, axis=1)
                found = jnp.dot(ones, both, preferred_element_type=jnp.float32).astype(jnp.bfloat16)
                for pair in range(ENTRIES // 2):
                    for side in range(2):
                        line = 2 * (n + side * TILES)
                        tiles[i * (step // 2) + group * (ENTRIES // 2) + pair, line : line + 2 * TILES] = found[
                            pair * 2 * TILES : (pair + 1) * 2 * TILES, side * lanes : (side + 1) * lanes
                        ]
        return carry

    lax.fori_loop(0, steps, some, 0)


def margin_tiles(margins, width):
    slots, partners, flat = margins.shape
    entries = slots * partners
    step = math.lcm(partners, ENTRIES)
    tiles = pl.pallas_call(
        margin_kernel,
        in_specs=[VMEM, ANY],
        out_specs=VMEM,
        out_shape=jax.ShapeDtypeStruct((entries // 2, width, 2 * width), jnp.bfloat16),
        scratch_shapes=[
            pltpu.VMEM((entries // step, step, flat), jnp.bfloat16),
            pltpu.SemaphoreType.DMA((entries // step,)),
        ],
        cost_estimate=pl.CostEstimate(flops=0, bytes_accessed=4 * margins.size, transcendentals=0),
        compiler_params=pltpu.CompilerParams(vmem_limit_bytes=12 * 2**20),
        name="margin_tiles",
    )(picker(), margins.reshape(entries, flat))
    return tiles.reshape(slots, partners // 2, width, 2 * width)


def couple_kernel(last, pieces, twist, partners, slot_of, *refs):
    gathered, refs = refs[:pieces], refs[pieces:]
    held, right, denom, mask, current = refs[:5]
    outs, refs = refs[5:7], refs[7:]
    expanded, halves, coupled = refs[:3]
    slots, pairs, width, lanes = held.shape
    half = slots // 2

    left = left_lanes(width)
    right_half = jnp.logical_not(left)
    base = 0
    for piece in gathered:
        held_devices = piece.shape[0] // half

        def expand(i, carry, piece=piece, base=base):
            tile = piece[i]
            at = 2 * (base * half + i)
            expanded[at] = tile
            expanded[at + 1] = swap_halves(tile)
            return carry

        lax.fori_loop(0, piece.shape[0], expand, 0, unroll=4)
        base += held_devices

    turn = twist[0] * slots

    def block(s, k):
        target = slot_of[partners[s, k]] ^ turn
        device, slot = target // slots, target % slots
        side = jnp.where(slot >= half, 1, 0)
        tile = expanded[2 * (device * half + slot - half * side) + (side ^ (k % 2))]
        return jnp.where(left if k % 2 == 0 else right_half, tile, jnp.zeros_like(tile))

    zero = jnp.zeros((lanes, lanes), jnp.bfloat16)

    def one_slot(s, at):
        for q in range(pairs // 2):
            upper = jnp.concatenate([block(s, 4 * q), block(s, 4 * q + 1)], axis=0)
            lower = jnp.concatenate([block(s, 4 * q + 2), block(s, 4 * q + 3)], axis=0)
            weights = jnp.concatenate(
                [jnp.concatenate([upper, zero], axis=1), jnp.concatenate([zero, lower], axis=1)], axis=0
            )
            margin = jnp.concatenate([held[s, 2 * q], held[s, 2 * q + 1]], axis=1)
            product = jnp.dot(margin, weights, preferred_element_type=jnp.float32)
            halves[at, :, 2 * q * lanes : 2 * (q + 1) * lanes] = product.astype(jnp.bfloat16)
        margin = jnp.concatenate([held[s, k] for k in range(pairs)], axis=1)
        coupled[s] = lax.dot_general(halves[at], margin, NT, preferred_element_type=jnp.float32)

    def some_slots(i, carry):
        for at in range(SLOTS_AT_ONCE):
            one_slot(i * SLOTS_AT_ONCE + at, at)
        return carry

    lax.fori_loop(0, slots // SLOTS_AT_ONCE, some_slots, 0)

    if last:
        store = refs[3]
    for u in range(half):
        both = jnp.concatenate([coupled[u], coupled[u + half]], axis=1)
        before = current[u]
        residual = mask[u] * (right[u] - denom[u] * before - both)
        after = before + residual / denom[u]
        if last:
            for n, tile in enumerate((after, residual)):
                store[2 * n, u * width : (u + 1) * width] = tile
                store[2 * n + 1, u * width : (u + 1) * width] = swap_halves(tile)
        else:
            outs[0][u] = after
            outs[1][u] = after.astype(jnp.bfloat16)
    if last:
        keep = lax.broadcasted_iota(jnp.int32, (half, lanes), 1) < width
        for n, out in enumerate(outs):
            for j in range(width // 2):
                upper = store[2 * n, pl.ds(2 * j, half, stride=width), :]
                lower = store[2 * n, pl.ds(2 * j + 1, half, stride=width), :]
                upper_turned = store[2 * n + 1, pl.ds(2 * j, half, stride=width), :]
                lower_turned = store[2 * n + 1, pl.ds(2 * j + 1, half, stride=width), :]
                out[:half, j * lanes : (j + 1) * lanes] = jnp.where(keep, upper, lower_turned)
                out[half:, j * lanes : (j + 1) * lanes] = jnp.where(keep, upper_turned, lower)


def couple(last, twist, partners, slot_of, gathered, margins, right, denom, mask, current):
    slots, pairs, width, lanes = margins.shape
    half = slots // 2
    devices = sum(piece.shape[0] for piece in gathered) // half
    packed = jax.ShapeDtypeStruct((half, width, lanes), jnp.float32)
    flat = jax.ShapeDtypeStruct((slots, width * width), jnp.float32)
    blocks = jax.ShapeDtypeStruct((half, width, lanes), jnp.bfloat16)
    outs = [flat, flat] if last else [packed, blocks]
    scratch = [
        pltpu.VMEM((devices * slots, width, lanes), jnp.bfloat16),
        pltpu.VMEM((SLOTS_AT_ONCE, width, pairs * lanes), jnp.bfloat16),
        pltpu.VMEM((slots, width, width), jnp.float32),
    ]
    if last:
        scratch.append(pltpu.VMEM((4, half * width, lanes), jnp.float32))
    operands = [*gathered, margins, right, denom, mask, current]
    size = sum(math.prod(x.shape) * x.dtype.itemsize for x in operands + outs + scratch)
    return pl.pallas_call(
        functools.partial(couple_kernel, last, len(gathered)),
        in_specs=[SMEM] * 3 + [VMEM] * len(operands),
        out_specs=[VMEM] * len(outs),
        out_shape=outs,
        scratch_shapes=scratch,
        compiler_params=pltpu.CompilerParams(vmem_limit_bytes=size + 4 * 2**20),
        name="couple",
    )(twist, partners, slot_of, *operands)


def gather(blocks, devices, meanwhile):
    if devices != 16:
        return [lax.all_gather(blocks, "pair", axis=0, tiled=True)], jnp.zeros((1,), jnp.int32), meanwhile

    def swap(piece, other):
        return lax.ppermute(piece, "pair", [(i, i ^ other) for i in range(devices)])

    piece = {0: blocks}
    for other in (2, 4, 12):
        piece[other] = swap(blocks, other)
    piece[6] = swap(piece[4], 2)
    piece[12], piece[6], meanwhile = lax.optimization_barrier((piece[12], piece[6], meanwhile))
    piece[8] = swap(piece[12], 4)
    piece[14] = swap(piece[12], 2)
    piece[10] = swap(piece[12], 6)
    for other in (0, 2, 4, 12):
        piece[other ^ 1] = swap(piece[other], 1)
    for other in (6, 14, 8, 10):
        piece[other ^ 1] = swap(piece[other], 1)
    return [piece[i] for i in range(devices)], lax.axis_index("pair").astype(jnp.int32).reshape(1), meanwhile


def shards(right_side, pno_energy, occ_energy, pno_count, margins, partners, slot_of):
    devices = lax.axis_size("pair")
    right, denom, mask, current, blocks = start(right_side, pno_energy, occ_energy, pno_count)
    tiles = margin_tiles(margins, pno_energy.shape[1])
    for step in range(ITERS):
        gathered, twist, tiles = gather(blocks, devices, tiles)
        outs = couple(step == ITERS - 1, twist, partners, slot_of, gathered, tiles, right, denom, mask, current)
        if step < ITERS - 1:
            current, blocks = outs
    return tuple(outs)


def solution(mesh):
    placed = (
        P(("groups", "pair"), None),
        P(("groups", "pair"), None),
        P(("groups", "pair")),
        P(("groups", "pair")),
        P(("groups", "pair"), None, None),
        P(("groups", "pair"), None),
        P("groups"),
    )
    return jax.shard_map(
        shards,
        mesh=mesh,
        in_specs=placed,
        out_specs=(P(("groups", "pair"), None), P(("groups", "pair"), None)),
        check_vma=False,
    )
```

```python
import functools
import math

import jax
import jax.numpy as jnp
import numpy as np
from jax import lax
from jax.experimental import pallas as pl
from jax.experimental.pallas import tpu as pltpu
from jax.sharding import PartitionSpec as P

ITERS = 2
FREQUENCY = 0.25
SLOTS_AT_ONCE = 8
ENTRIES = 16
TILES = 8
NT = (((1,), (1,)), ((), ()))
VMEM = pl.BlockSpec(memory_space=pltpu.VMEM)
SMEM = pl.BlockSpec(memory_space=pltpu.SMEM)
HBM = pl.BlockSpec(memory_space=pltpu.HBM)


def left_lanes(width):
    return lax.broadcasted_iota(jnp.int32, (width, 2 * width), 1) < width


def swap_halves(tile):
    width = tile.shape[1] // 2
    return jnp.concatenate([tile[:, width:], tile[:, :width]], axis=1)


def begin(count, occ, right, energy, rows):
    slots, width = energy.shape
    half = slots // 2
    lanes = 2 * width
    slot = lax.broadcasted_iota(jnp.int32, (slots, lanes), 0)
    for j in range(width // 2):
        part = right[:, j * lanes : (j + 1) * lanes]
        turned = swap_halves(part)
        rows[pl.ds(2 * j, slots, stride=width), :] = jnp.where(slot < half, part, turned)
        rows[pl.ds(2 * j + 1, slots, stride=width), :] = jnp.where(slot < half, turned, part)
    left = left_lanes(width)
    row = lax.broadcasted_iota(jnp.int32, (width, lanes), 0)
    column = lax.broadcasted_iota(jnp.int32, (width, lanes), 1) % width
    across = energy[...]
    down = across.T
    for u in range(half):
        v = u + half
        first = jnp.broadcast_to(down[:, u : u + 1], (width, lanes))
        second = jnp.broadcast_to(down[:, v : v + 1], (width, lanes))
        along = jnp.concatenate([across[u : u + 1], across[v : v + 1]], axis=1)
        shift = jnp.where(left, occ[u], occ[v])
        denom = jnp.where(left, first, second) + along - shift - FREQUENCY
        most = jnp.where(left, count[u], count[v])
        mask = jnp.where((row < most) & (column < most), 1.0, 0.0)
        yield u, jnp.where(left, rows[u * width : (u + 1) * width], rows[v * width : (v + 1) * width]), denom, mask


def start_kernel(count, occ, right, energy, blocks_out, rows):
    for u, tile, denom, mask in begin(count, occ, right, energy, rows):
        blocks_out[u] = (mask * tile / denom).astype(jnp.bfloat16)


def state_kernel(count, occ, twist, partners, slot_of, right, energy, right_out, denom_out, mask_out, solution_out, place_out, rows):
    for u, tile, denom, mask in begin(count, occ, right, energy, rows):
        right_out[u] = tile
        denom_out[u] = denom
        mask_out[u] = mask
        solution_out[u] = mask * tile / denom
    slots, entries = partners.shape
    half = slots // 2

    def places(s, carry):
        for k in range(entries):
            target = slot_of[partners[s, k]] ^ (twist[0] * slots)
            slot = lax.rem(target, slots)
            side = lax.div(slot, half)
            tile = lax.div(target, slots) * half + slot - side * half
            place_out[s, k] = 4 * tile + 2 * side + k % 2
        return carry

    lax.fori_loop(0, slots, places, 0)


def start(right_side, pno_energy, occ_energy, pno_count):
    slots, width = pno_energy.shape
    return pl.pallas_call(
        start_kernel,
        in_specs=[SMEM, SMEM, VMEM, VMEM],
        out_specs=VMEM,
        out_shape=jax.ShapeDtypeStruct((slots // 2, width, 2 * width), jnp.bfloat16),
        scratch_shapes=[pltpu.VMEM((slots * width, 2 * width), jnp.float32)],
        name="start",
    )(pno_count, occ_energy, right_side, pno_energy)


def state(twist, partners, slot_of, right_side, pno_energy, occ_energy, pno_count):
    slots, width = pno_energy.shape
    tiles = jax.ShapeDtypeStruct((slots // 2, width, 2 * width), jnp.float32)
    return pl.pallas_call(
        state_kernel,
        in_specs=[SMEM] * 5 + [VMEM] * 2,
        out_specs=[VMEM] * 4 + [SMEM],
        out_shape=[tiles] * 4 + [jax.ShapeDtypeStruct(partners.shape, jnp.int32)],
        scratch_shapes=[pltpu.VMEM((slots * width, 2 * width), jnp.float32)],
        cost_estimate=pl.CostEstimate(flops=0, bytes_accessed=32 * right_side.size, transcendentals=0),
        name="state",
    )(pno_count, occ_energy, twist, partners, slot_of, right_side, pno_energy)


def picker():
    pair, line = np.divmod(np.arange(ENTRIES * TILES), 2 * TILES)
    ones = np.zeros((ENTRIES * TILES, 2 * TILES * ENTRIES), np.float32)
    for side in range(2):
        ones[np.arange(ENTRIES * TILES), (line % 2) * TILES * ENTRIES + (line // 2) * ENTRIES + 2 * pair + side] = 1
    return jnp.asarray(ones, jnp.bfloat16)


def margin_kernel(pick, margins, tiles, held, made, arrived, left_for):
    width, lanes = tiles.shape[1:]
    steps, step = held.shape[:2]
    left = lax.broadcasted_iota(jnp.int32, (ENTRIES, lanes), 1) < width
    even = lax.broadcasted_iota(jnp.int32, (ENTRIES, lanes), 0) % 2 == 0

    def fetch(i):
        return pltpu.make_async_copy(margins.at[pl.ds(i * step, step)], held.at[i], arrived.at[i])

    def store(i):
        return pltpu.make_async_copy(made.at[i], tiles.at[pl.ds(i * (step // 2), step // 2)], left_for.at[i])

    for i in range(steps):
        fetch(i).start()
    ones = pick[...]

    def some(i, carry):
        fetch(i).wait()
        for group in range(step // ENTRIES):
            rows = slice(group * ENTRIES, (group + 1) * ENTRIES)
            for n in range(0, width // 2, 2 * TILES):
                sides = []
                for part in (n, n + TILES):
                    upper, lower = [], []
                    for j in range(part, part + TILES):
                        here = held[i, rows, j * lanes : (j + 1) * lanes]
                        turned = swap_halves(here)
                        zero = jnp.zeros_like(here)
                        upper.append(jnp.where(left & even, here, jnp.where(left | even, zero, turned)))
                        lower.append(jnp.where(left & even, turned, jnp.where(left | even, zero, here)))
                    sides.append(jnp.concatenate(upper + lower, axis=0))
                both = jnp.concatenate(sides, axis=1)
                found = jnp.dot(ones, both, preferred_element_type=jnp.float32).astype(jnp.bfloat16)
                for pair in range(ENTRIES // 2):
                    for side in range(2):
                        line = 2 * (n + side * TILES)
                        made[i, group * (ENTRIES // 2) + pair, line : line + 2 * TILES] = found[
                            pair * 2 * TILES : (pair + 1) * 2 * TILES, side * lanes : (side + 1) * lanes
                        ]
        store(i).start()
        return carry

    lax.fori_loop(0, steps, some, 0)
    for i in range(steps):
        store(i).wait()


def margin_tiles(margins, width):
    slots, partners, flat = margins.shape
    entries = slots * partners
    step = math.lcm(partners, ENTRIES)
    tiles = pl.pallas_call(
        margin_kernel,
        in_specs=[VMEM, HBM],
        out_specs=HBM,
        out_shape=jax.ShapeDtypeStruct((entries // 2, width, 2 * width), jnp.bfloat16),
        scratch_shapes=[
            pltpu.VMEM((entries // step, step, flat), jnp.bfloat16),
            pltpu.VMEM((entries // step, step // 2, width, 2 * width), jnp.bfloat16),
            pltpu.SemaphoreType.DMA((entries // step,)),
            pltpu.SemaphoreType.DMA((entries // step,)),
        ],
        cost_estimate=pl.CostEstimate(flops=0, bytes_accessed=4 * margins.size, transcendentals=0),
        compiler_params=pltpu.CompilerParams(vmem_limit_bytes=4 * margins.size + 2**20),
        name="margin_tiles",
    )(picker(), margins.reshape(entries, flat))
    return tiles.reshape(slots, partners // 2, width, 2 * width)


def couple_kernel(last, pieces, place, *refs):
    gathered, refs = refs[:pieces], refs[pieces:]
    margins, right, denom, mask, current = refs[:5]
    outs, refs = refs[5:7], refs[7:]
    expanded, held, halves, coupled, arrived = refs[-5:]
    slots, pairs, width, lanes = held.shape
    half = slots // 2

    def fetch(i):
        some = pl.ds(i * SLOTS_AT_ONCE, SLOTS_AT_ONCE)
        return pltpu.make_async_copy(margins.at[some], held.at[some], arrived.at[i])

    for i in range(slots // SLOTS_AT_ONCE):
        fetch(i).start()

    left = left_lanes(width)
    at = 0
    for piece in gathered:

        def expand(i, at, piece=piece):
            tile = piece[i]
            turned = swap_halves(tile)
            zero = jnp.zeros_like(tile)
            expanded[at] = jnp.where(left, tile, zero)
            expanded[at + 1] = jnp.where(left, zero, turned)
            expanded[at + 2] = jnp.where(left, turned, zero)
            expanded[at + 3] = jnp.where(left, zero, tile)
            return at + 4

        at = lax.fori_loop(0, piece.shape[0], expand, at, unroll=half)

    def one_slot(s, at):
        for k in range(pairs):
            weights = jnp.concatenate([expanded[place[s, 2 * k]], expanded[place[s, 2 * k + 1]]], axis=0)
            product = jnp.dot(held[s, k], weights, preferred_element_type=jnp.float32)
            halves[at, :, k * lanes : (k + 1) * lanes] = product.astype(jnp.bfloat16)
        margin = jnp.concatenate([held[s, k] for k in range(pairs)], axis=1)
        coupled[s] = lax.dot_general(halves[at], margin, NT, preferred_element_type=jnp.float32)

    def some_slots(i, carry):
        fetch(i).wait()
        for at in range(SLOTS_AT_ONCE):
            one_slot(i * SLOTS_AT_ONCE + at, at)
        return carry

    lax.fori_loop(0, slots // SLOTS_AT_ONCE, some_slots, 0)

    if last:
        store = refs[0]
    for u in range(half):
        both = jnp.concatenate([coupled[u], coupled[u + half]], axis=1)
        before = current[u]
        residual = mask[u] * (right[u] - denom[u] * before - both)
        after = before + residual / denom[u]
        if last:
            for n, tile in enumerate((after, residual)):
                store[2 * n, u * width : (u + 1) * width] = tile
                store[2 * n + 1, u * width : (u + 1) * width] = swap_halves(tile)
        else:
            outs[0][u] = after
            outs[1][u] = after.astype(jnp.bfloat16)
    if last:
        keep = lax.broadcasted_iota(jnp.int32, (half, lanes), 1) < width
        for n, out in enumerate(outs):
            for j in range(width // 2):
                upper = store[2 * n, pl.ds(2 * j, half, stride=width), :]
                lower = store[2 * n, pl.ds(2 * j + 1, half, stride=width), :]
                upper_turned = store[2 * n + 1, pl.ds(2 * j, half, stride=width), :]
                lower_turned = store[2 * n + 1, pl.ds(2 * j + 1, half, stride=width), :]
                out[:half, j * lanes : (j + 1) * lanes] = jnp.where(keep, upper, lower_turned)
                out[half:, j * lanes : (j + 1) * lanes] = jnp.where(keep, upper_turned, lower)


def couple(last, place, gathered, margins, right, denom, mask, current):
    slots, pairs, width, lanes = margins.shape
    half = slots // 2
    devices = sum(piece.shape[0] for piece in gathered) // half
    packed = jax.ShapeDtypeStruct((half, width, lanes), jnp.float32)
    flat = jax.ShapeDtypeStruct((slots, width * width), jnp.float32)
    blocks = jax.ShapeDtypeStruct((half, width, lanes), jnp.bfloat16)
    outs = [flat, flat] if last else [packed, blocks]
    scratch = [
        pltpu.VMEM((2 * devices * slots, width, lanes), jnp.bfloat16),
        pltpu.VMEM((slots, pairs, width, lanes), jnp.bfloat16),
        pltpu.VMEM((SLOTS_AT_ONCE, width, pairs * lanes), jnp.bfloat16),
        pltpu.VMEM((slots, width, width), jnp.float32),
    ]
    if last:
        scratch.insert(0, pltpu.VMEM((4, half * width, lanes), jnp.float32))
    operands = [*gathered, margins, right, denom, mask, current]
    size = sum(math.prod(x.shape) * x.dtype.itemsize for x in operands + outs + scratch)
    scratch.append(pltpu.SemaphoreType.DMA((slots // SLOTS_AT_ONCE,)))
    return pl.pallas_call(
        functools.partial(couple_kernel, last, len(gathered)),
        in_specs=[SMEM] + [VMEM] * len(gathered) + [HBM] + [VMEM] * 4,
        out_specs=[VMEM] * len(outs),
        out_shape=outs,
        scratch_shapes=scratch,
        compiler_params=pltpu.CompilerParams(vmem_limit_bytes=size + 4 * 2**20),
        name="couple",
    )(place, *operands)


def gather(blocks, devices, meanwhile):
    if devices != 16:
        return [lax.all_gather(blocks, "pair", axis=0, tiled=True)], meanwhile

    def swap(piece, other):
        return lax.ppermute(piece, "pair", [(i, i ^ other) for i in range(devices)])

    first, second = meanwhile
    piece = {0: blocks}
    for other in (2, 4, 12):
        piece[other] = swap(blocks, other)
    piece[6] = swap(piece[4], 2)
    piece[12], piece[6], first = lax.optimization_barrier((piece[12], piece[6], first))
    piece[8] = swap(piece[12], 4)
    piece[14] = swap(piece[12], 2)
    piece[10] = swap(piece[12], 6)
    for other in (0, 2, 4, 12, 6):
        piece[other ^ 1] = swap(piece[other], 1)
    piece[14], second = lax.optimization_barrier((piece[14], second))
    for other in (14, 8, 10):
        piece[other ^ 1] = swap(piece[other], 1)
    return [piece[i] for i in range(devices)], (first, second)


def shards(right_side, pno_energy, occ_energy, pno_count, margins, partners, slot_of):
    devices = lax.axis_size("pair")
    twist = lax.axis_index("pair") if devices == 16 else 0
    twist = jnp.full((1,), twist, jnp.int32)
    blocks = start(right_side, pno_energy, occ_energy, pno_count)
    tiles = margin_tiles(margins, pno_energy.shape[1])
    states = state(twist, partners, slot_of, right_side, pno_energy, occ_energy, pno_count)
    for step in range(ITERS):
        gathered, (tiles, states) = gather(blocks, devices, (tiles, states))
        right, denom, mask, current, place = states
        outs = couple(step == ITERS - 1, place, gathered, tiles, right, denom, mask, current)
        if step < ITERS - 1:
            current, blocks = outs
            states = right, denom, mask, current, place
    return tuple(outs)


def solution(mesh):
    placed = (
        P(("groups", "pair"), None),
        P(("groups", "pair"), None),
        P(("groups", "pair")),
        P(("groups", "pair")),
        P(("groups", "pair"), None, None),
        P(("groups", "pair"), None),
        P("groups"),
    )
    return jax.shard_map(
        shards,
        mesh=mesh,
        in_specs=placed,
        out_specs=(P(("groups", "pair"), None), P(("groups", "pair"), None)),
        check_vma=False,
    )
```

```python
import functools
import math

import jax
import jax.numpy as jnp
import numpy as np
from jax import lax
from jax.experimental import pallas as pl
from jax.experimental.pallas import tpu as pltpu
from jax.sharding import PartitionSpec as P

FREQUENCY = 0.25
SLOTS_AT_ONCE = 8
ENTRIES = 16
TILES = 8
NT = (((1,), (1,)), ((), ()))
VMEM = pl.BlockSpec(memory_space=pltpu.VMEM)
SMEM = pl.BlockSpec(memory_space=pltpu.SMEM)
VMEM_LIMIT = 58 * 2**20
STATE_ROOM = 16
COUPLE_LIMIT = 50 * 2**20
HBM = pl.BlockSpec(memory_space=pltpu.HBM)


def left_lanes(width):
    return lax.broadcasted_iota(jnp.int32, (width, 2 * width), 1) < width


def swap_halves(tile):
    width = tile.shape[1] // 2
    return jnp.concatenate([tile[:, width:], tile[:, :width]], axis=1)


def begin(count, occ, right, energy, rows):
    slots, width = energy.shape
    half = slots // 2
    lanes = 2 * width
    slot = lax.broadcasted_iota(jnp.int32, (slots, lanes), 0)
    for j in range(width // 2):
        part = right[:, j * lanes : (j + 1) * lanes]
        turned = swap_halves(part)
        rows[pl.ds(2 * j, slots, stride=width), :] = jnp.where(slot < half, part, turned)
        rows[pl.ds(2 * j + 1, slots, stride=width), :] = jnp.where(slot < half, turned, part)
    left = left_lanes(width)
    row = lax.broadcasted_iota(jnp.int32, (width, lanes), 0)
    column = lax.broadcasted_iota(jnp.int32, (width, lanes), 1) % width
    across = energy[...]
    down = across.T
    for u in range(half):
        v = u + half
        first = jnp.broadcast_to(down[:, u : u + 1], (width, lanes))
        second = jnp.broadcast_to(down[:, v : v + 1], (width, lanes))
        along = jnp.concatenate([across[u : u + 1], across[v : v + 1]], axis=1)
        shift = jnp.where(left, occ[u], occ[v])
        denom = jnp.where(left, first, second) + along - shift - FREQUENCY
        most = jnp.where(left, count[u], count[v])
        mask = jnp.where((row < most) & (column < most), 1.0, 0.0)
        yield u, jnp.where(left, rows[u * width : (u + 1) * width], rows[v * width : (v + 1) * width]), denom, mask


def start_kernel(count, occ, right, energy, blocks_out, rows):
    for u, tile, denom, mask in begin(count, occ, right, energy, rows):
        blocks_out[u] = (mask * tile / denom).astype(jnp.bfloat16)


def state_kernel(count, occ, right, energy, out_hbm, rows, out, done):
    for u, tile, denom, mask in begin(count, occ, right, energy, rows):
        out[0, u] = tile
        out[1, u] = denom
        out[2, u] = mask
        out[3, u] = mask * tile / denom
    copy = pltpu.make_async_copy(out, out_hbm.at[:4], done)
    copy.start()
    copy.wait()


def start(right_side, pno_energy, occ_energy, pno_count):
    slots, width = pno_energy.shape
    return pl.pallas_call(
        start_kernel,
        in_specs=[SMEM, SMEM, VMEM, VMEM],
        out_specs=VMEM,
        out_shape=jax.ShapeDtypeStruct((slots // 2, width, 2 * width), jnp.bfloat16),
        scratch_shapes=[pltpu.VMEM((slots * width, 2 * width), jnp.float32)],
        name="start",
    )(pno_count, occ_energy, right_side, pno_energy)


def state(right_side, pno_energy, occ_energy, pno_count):
    slots, width = pno_energy.shape
    return pl.pallas_call(
        state_kernel,
        in_specs=[SMEM] * 2 + [VMEM] * 2,
        out_specs=HBM,
        out_shape=jax.ShapeDtypeStruct((STATE_ROOM, slots // 2, width, 2 * width), jnp.float32),
        scratch_shapes=[
            pltpu.VMEM((slots * width, 2 * width), jnp.float32),
            pltpu.VMEM((4, slots // 2, width, 2 * width), jnp.float32),
            pltpu.SemaphoreType.DMA,
        ],
        cost_estimate=pl.CostEstimate(flops=0, bytes_accessed=32 * right_side.size, transcendentals=0),
        compiler_params=pltpu.CompilerParams(vmem_limit_bytes=VMEM_LIMIT),
        name="state",
    )(pno_count, occ_energy, right_side, pno_energy)


def places(slot_of, slots, twist):
    half = slots // 2
    device, slot = slot_of // slots, slot_of % slots
    return 4 * ((device ^ twist) * half + slot % half) + 2 * (slot // half)


def picker():
    pair, line = np.divmod(np.arange(ENTRIES * TILES), 2 * TILES)
    ones = np.zeros((ENTRIES * TILES, 2 * TILES * ENTRIES), np.float32)
    for side in range(2):
        ones[np.arange(ENTRIES * TILES), (line % 2) * TILES * ENTRIES + (line // 2) * ENTRIES + 2 * pair + side] = 1
    return jnp.asarray(ones, jnp.bfloat16)


def margin_kernel(pick, margins, tiles, held, made, arrived, left_for):
    width, lanes = tiles.shape[1:]
    steps, step = held.shape[:2]
    left = lax.broadcasted_iota(jnp.int32, (ENTRIES, lanes), 1) < width
    even = lax.broadcasted_iota(jnp.int32, (ENTRIES, lanes), 0) % 2 == 0

    def fetch(i):
        return pltpu.make_async_copy(margins.at[pl.ds(i * step, step)], held.at[i], arrived.at[i])

    def store(i):
        return pltpu.make_async_copy(made.at[i], tiles.at[pl.ds(i * (step // 2), step // 2)], left_for.at[i])

    for i in range(steps):
        fetch(i).start()
    ones = pick[...]

    def some(i, carry):
        fetch(i).wait()
        for group in range(step // ENTRIES):
            rows = slice(group * ENTRIES, (group + 1) * ENTRIES)
            for n in range(0, width // 2, 2 * TILES):
                sides = []
                for part in (n, n + TILES):
                    upper, lower = [], []
                    for j in range(part, part + TILES):
                        here = held[i, rows, j * lanes : (j + 1) * lanes]
                        turned = swap_halves(here)
                        zero = jnp.zeros_like(here)
                        upper.append(jnp.where(left & even, here, jnp.where(left | even, zero, turned)))
                        lower.append(jnp.where(left & even, turned, jnp.where(left | even, zero, here)))
                    sides.append(jnp.concatenate(upper + lower, axis=0))
                both = jnp.concatenate(sides, axis=1)
                found = jnp.dot(ones, both, preferred_element_type=jnp.float32).astype(jnp.bfloat16)
                for pair in range(ENTRIES // 2):
                    for side in range(2):
                        line = 2 * (n + side * TILES)
                        made[i, group * (ENTRIES // 2) + pair, line : line + 2 * TILES] = found[
                            pair * 2 * TILES : (pair + 1) * 2 * TILES, side * lanes : (side + 1) * lanes
                        ]
        store(i).start()
        return carry

    lax.fori_loop(0, steps, some, 0)
    for i in range(steps):
        store(i).wait()


def margin_tiles(margins, width):
    slots, partners, flat = margins.shape
    entries = slots * partners
    step = math.lcm(partners, ENTRIES)
    tiles = pl.pallas_call(
        margin_kernel,
        in_specs=[VMEM, HBM],
        out_specs=HBM,
        out_shape=jax.ShapeDtypeStruct((entries // 2, width, 2 * width), jnp.bfloat16),
        scratch_shapes=[
            pltpu.VMEM((entries // step, step, flat), jnp.bfloat16),
            pltpu.VMEM((entries // step, step // 2, width, 2 * width), jnp.bfloat16),
            pltpu.SemaphoreType.DMA((entries // step,)),
            pltpu.SemaphoreType.DMA((entries // step,)),
        ],
        cost_estimate=pl.CostEstimate(flops=0, bytes_accessed=4 * margins.size, transcendentals=0),
        compiler_params=pltpu.CompilerParams(vmem_limit_bytes=VMEM_LIMIT),
        name="margin_tiles",
    )(picker(), margins.reshape(entries, flat))
    return tiles.reshape(slots, partners // 2, width, 2 * width)


def couple_kernel(last, pieces, place, partners, *refs):
    gathered, refs = refs[:pieces], refs[pieces:]
    margins, state = refs[:2]
    refs = refs[2:]
    if last:
        current, refs = refs[0], refs[1:]
    outs, refs = refs[:2], refs[2:]
    expanded, held, halves, coupled, steady, arrived = refs[-6:]
    slots, pairs, width, lanes = held.shape
    half = slots // 2

    def fetch(i):
        some = pl.ds(i * SLOTS_AT_ONCE, SLOTS_AT_ONCE)
        return pltpu.make_async_copy(margins.at[some], held.at[some], arrived.at[i])

    fetch_state = pltpu.make_async_copy(state.at[:4], steady, arrived.at[slots // SLOTS_AT_ONCE])
    for i in range(slots // SLOTS_AT_ONCE):
        fetch(i).start()
    fetch_state.start()

    left = left_lanes(width)
    at = 0
    for piece in gathered:

        def expand(i, at, piece=piece):
            tile = piece[i]
            turned = swap_halves(tile)
            zero = jnp.zeros_like(tile)
            expanded[at] = jnp.where(left, tile, zero)
            expanded[at + 1] = jnp.where(left, zero, turned)
            expanded[at + 2] = jnp.where(left, turned, zero)
            expanded[at + 3] = jnp.where(left, zero, tile)
            return at + 4

        at = lax.fori_loop(0, piece.shape[0], expand, at, unroll=half)

    def one_slot(s, at):
        for k in range(pairs):
            first, second = place[partners[s, 2 * k]], place[partners[s, 2 * k + 1]] + 1
            weights = jnp.concatenate([expanded[first], expanded[second]], axis=0)
            product = jnp.dot(held[s, k], weights, preferred_element_type=jnp.float32)
            halves[at, :, k * lanes : (k + 1) * lanes] = product.astype(jnp.bfloat16)
        margin = jnp.concatenate([held[s, k] for k in range(pairs)], axis=1)
        coupled[s] = lax.dot_general(halves[at], margin, NT, preferred_element_type=jnp.float32)

    def some_slots(i, carry):
        fetch(i).wait()
        for at in range(SLOTS_AT_ONCE):
            one_slot(i * SLOTS_AT_ONCE + at, at)
        return carry

    lax.fori_loop(0, slots // SLOTS_AT_ONCE, some_slots, 0)

    if last:
        store = refs[0]
    fetch_state.wait()
    for u in range(half):
        both = jnp.concatenate([coupled[u], coupled[u + half]], axis=1)
        right, denom, mask = steady[0, u], steady[1, u], steady[2, u]
        before = current[u] if last else steady[3, u]
        residual = mask * (right - denom * before - both)
        after = before + residual / denom
        if last:
            for n, tile in enumerate((after, residual)):
                store[2 * n, u * width : (u + 1) * width] = tile
                store[2 * n + 1, u * width : (u + 1) * width] = swap_halves(tile)
        else:
            outs[0][u] = after
            outs[1][u] = after.astype(jnp.bfloat16)
    if last:
        keep = lax.broadcasted_iota(jnp.int32, (half, lanes), 1) < width
        for n, out in enumerate(outs):
            for j in range(width // 2):
                upper = store[2 * n, pl.ds(2 * j, half, stride=width), :]
                lower = store[2 * n, pl.ds(2 * j + 1, half, stride=width), :]
                upper_turned = store[2 * n + 1, pl.ds(2 * j, half, stride=width), :]
                lower_turned = store[2 * n + 1, pl.ds(2 * j + 1, half, stride=width), :]
                out[:half, j * lanes : (j + 1) * lanes] = jnp.where(keep, upper, lower_turned)
                out[half:, j * lanes : (j + 1) * lanes] = jnp.where(keep, upper_turned, lower)


def couple(place, partners, gathered, margins, state, current):
    last = current is not None
    slots, pairs, width, lanes = margins.shape
    half = slots // 2
    devices = sum(piece.shape[0] for piece in gathered) // half
    packed = jax.ShapeDtypeStruct((half, width, lanes), jnp.float32)
    flat = jax.ShapeDtypeStruct((slots, width * width), jnp.float32)
    blocks = jax.ShapeDtypeStruct((half, width, lanes), jnp.bfloat16)
    outs = [flat, flat] if last else [packed, blocks]
    scratch = [
        pltpu.VMEM((2 * devices * slots, width, lanes), jnp.bfloat16),
        pltpu.VMEM((slots, pairs, width, lanes), jnp.bfloat16),
        pltpu.VMEM((SLOTS_AT_ONCE, width, pairs * lanes), jnp.bfloat16),
        pltpu.VMEM((slots, width, width), jnp.float32),
    ]
    if last:
        scratch.insert(0, pltpu.VMEM((4, half * width, lanes), jnp.float32))
    operands = [*gathered, margins, state] + [current] * last
    scratch.append(pltpu.VMEM((4, *state.shape[1:]), jnp.float32))
    scratch.append(pltpu.SemaphoreType.DMA((slots // SLOTS_AT_ONCE + 1,)))
    return pl.pallas_call(
        functools.partial(couple_kernel, last, len(gathered)),
        in_specs=[SMEM] * 2 + [VMEM] * len(gathered) + [HBM] * 2 + [VMEM] * last,
        out_specs=[VMEM] * len(outs),
        out_shape=outs,
        scratch_shapes=scratch,
        compiler_params=pltpu.CompilerParams(vmem_limit_bytes=COUPLE_LIMIT),
        name="couple",
    )(place, partners, *operands)


def gather(blocks, devices, meanwhile):
    if devices != 16:
        return [lax.all_gather(blocks, "pair", axis=0, tiled=True)], meanwhile

    def swap(piece, other):
        return lax.ppermute(piece, "pair", [(i, i ^ other) for i in range(devices)])

    first, second = meanwhile
    piece = {0: blocks}
    for other in (2, 4, 12):
        piece[other] = swap(blocks, other)
    piece[12], first = lax.optimization_barrier((piece[12], first))
    piece[8] = swap(piece[12], 4)
    piece[10] = swap(piece[12], 6)
    piece[14] = swap(piece[12], 2)
    piece[6] = swap(piece[4], 2)
    piece[10], second = lax.optimization_barrier((piece[10], second))
    for other in (0, 2, 4, 12, 6, 14, 8, 10):
        piece[other ^ 1] = swap(piece[other], 1)
    return [piece[i] for i in range(devices)], (first, second)


def shards(right_side, pno_energy, occ_energy, pno_count, margins, partners, slot_of):
    devices = lax.axis_size("pair")
    place = places(slot_of, partners.shape[0], lax.axis_index("pair") if devices == 16 else 0)
    blocks = start(right_side, pno_energy, occ_energy, pno_count)
    tiles = margin_tiles(margins, pno_energy.shape[1])
    steady = state(right_side, pno_energy, occ_energy, pno_count)
    gathered, (tiles, steady) = gather(blocks, devices, (tiles, steady))
    current, blocks = couple(place, partners, gathered, tiles, steady, None)
    gathered, (tiles, steady) = gather(blocks, devices, (tiles, steady))
    return tuple(couple(place, partners, gathered, tiles, steady, current))


def solution(mesh):
    placed = (
        P(("groups", "pair"), None),
        P(("groups", "pair"), None),
        P(("groups", "pair")),
        P(("groups", "pair")),
        P(("groups", "pair"), None, None),
        P(("groups", "pair"), None),
        P("groups"),
    )
    return jax.shard_map(
        shards,
        mesh=mesh,
        in_specs=placed,
        out_specs=(P(("groups", "pair"), None), P(("groups", "pair"), None)),
        check_vma=False,
    )
```

```python
import functools
import math

import jax
import jax.numpy as jnp
import numpy as np
from jax import lax
from jax.experimental import pallas as pl
from jax.experimental.pallas import tpu as pltpu
from jax.sharding import PartitionSpec as P

FREQUENCY = 0.25
SLOTS_AT_ONCE = 8
ENTRIES = 16
TILES = 8
FIRST = 6
AHEAD = 4
CUTS = 2
NT = (((1,), (1,)), ((), ()))
VMEM = pl.BlockSpec(memory_space=pltpu.VMEM)
SMEM = pl.BlockSpec(memory_space=pltpu.SMEM)
VMEM_LIMIT = 58 * 2**20
STATE_ROOM = 16
COUPLE_LIMIT = 50 * 2**20
HBM = pl.BlockSpec(memory_space=pltpu.HBM)


def left_lanes(width):
    return lax.broadcasted_iota(jnp.int32, (width, 2 * width), 1) < width


def swap_halves(tile):
    width = tile.shape[1] // 2
    return jnp.concatenate([tile[:, width:], tile[:, :width]], axis=1)


def begin(count, occ, right, energy, rows):
    slots, width = energy.shape
    half = slots // 2
    lanes = 2 * width
    slot = lax.broadcasted_iota(jnp.int32, (slots, lanes), 0)
    for j in range(width // 2):
        part = right[:, j * lanes : (j + 1) * lanes]
        turned = swap_halves(part)
        rows[pl.ds(2 * j, slots, stride=width), :] = jnp.where(slot < half, part, turned)
        rows[pl.ds(2 * j + 1, slots, stride=width), :] = jnp.where(slot < half, turned, part)
    left = left_lanes(width)
    row = lax.broadcasted_iota(jnp.int32, (width, lanes), 0)
    column = lax.broadcasted_iota(jnp.int32, (width, lanes), 1) % width
    across = energy[...]
    down = across.T
    for u in range(half):
        v = u + half
        first = jnp.broadcast_to(down[:, u : u + 1], (width, lanes))
        second = jnp.broadcast_to(down[:, v : v + 1], (width, lanes))
        along = jnp.concatenate([across[u : u + 1], across[v : v + 1]], axis=1)
        shift = jnp.where(left, occ[u], occ[v])
        denom = jnp.where(left, first, second) + along - shift - FREQUENCY
        most = jnp.where(left, count[u], count[v])
        mask = jnp.where((row < most) & (column < most), 1.0, 0.0)
        yield u, jnp.where(left, rows[u * width : (u + 1) * width], rows[v * width : (v + 1) * width]), denom, mask


def start_kernel(count, occ, right, energy, blocks_out, rows):
    for u, tile, denom, mask in begin(count, occ, right, energy, rows):
        blocks_out[u] = (mask * tile / denom).astype(jnp.bfloat16)


def start(right_side, pno_energy, occ_energy, pno_count):
    slots, width = pno_energy.shape
    return pl.pallas_call(
        start_kernel,
        in_specs=[SMEM, SMEM, VMEM, VMEM],
        out_specs=VMEM,
        out_shape=jax.ShapeDtypeStruct((slots // 2, width, 2 * width), jnp.bfloat16),
        scratch_shapes=[pltpu.VMEM((slots * width, 2 * width), jnp.float32)],
        name="start",
    )(pno_count, occ_energy, right_side, pno_energy)


def places(slot_of, slots, twist):
    half = slots // 2
    device, slot = slot_of // slots, slot_of % slots
    return 4 * ((device ^ twist) * half + slot % half) + 2 * (slot // half)


def picker():
    pair, line = np.divmod(np.arange(ENTRIES * TILES), 2 * TILES)
    ones = np.zeros((ENTRIES * TILES, 2 * TILES * ENTRIES), np.float32)
    for side in range(2):
        ones[np.arange(ENTRIES * TILES), (line % 2) * TILES * ENTRIES + (line // 2) * ENTRIES + 2 * pair + side] = 1
    return jnp.asarray(ones, jnp.bfloat16)


def repack(i, ones, held, made):
    step, width, lanes = held.shape[1], *made.shape[2:]
    left = lax.broadcasted_iota(jnp.int32, (ENTRIES, lanes), 1) < width
    even = lax.broadcasted_iota(jnp.int32, (ENTRIES, lanes), 0) % 2 == 0
    for group in range(step // ENTRIES):
        rows = slice(group * ENTRIES, (group + 1) * ENTRIES)
        for n in range(0, width // 2, 2 * TILES):
            sides = []
            for part in (n, n + TILES):
                upper, lower = [], []
                for j in range(part, part + TILES):
                    here = held[i, rows, j * lanes : (j + 1) * lanes]
                    turned = swap_halves(here)
                    zero = jnp.zeros_like(here)
                    upper.append(jnp.where(left & even, here, jnp.where(left | even, zero, turned)))
                    lower.append(jnp.where(left & even, turned, jnp.where(left | even, zero, here)))
                sides.append(jnp.concatenate(upper + lower, axis=0))
            both = jnp.concatenate(sides, axis=1)
            found = jnp.dot(ones, both, preferred_element_type=jnp.float32).astype(jnp.bfloat16)
            for pair in range(ENTRIES // 2):
                for side in range(2):
                    line = 2 * (n + side * TILES)
                    made[i, group * (ENTRIES // 2) + pair, line : line + 2 * TILES] = found[
                        pair * 2 * TILES : (pair + 1) * 2 * TILES, side * lanes : (side + 1) * lanes
                    ]


def margin_kernel(offset, pick, margins, *refs):
    if offset > 0:
        _, count, occ, right, energy, tiles, state, *refs, rows, out, done = refs
        refs = tiles, *refs
    tiles, held, made, arrived, left_for = refs
    steps, step = held.shape[:2]

    def fetch(i):
        return pltpu.make_async_copy(margins.at[pl.ds((offset + i) * step, step)], held.at[i], arrived.at[i])

    def store(i):
        some = pl.ds((offset + i) * (step // 2), step // 2)
        return pltpu.make_async_copy(made.at[i], tiles.at[some], left_for.at[i])

    for i in range(min(AHEAD, steps)):
        fetch(i).start()
    if offset > 0:
        for u, tile, denom, mask in begin(count, occ, right, energy, rows):
            out[0, u] = tile
            out[1, u] = denom
            out[2, u] = mask
            out[3, u] = mask * tile / denom
        state_copy = pltpu.make_async_copy(out, state.at[:4], done)
        state_copy.start()
    ones = pick[...]

    def some(i, carry):
        fetch(i).wait()

        @pl.when(i + AHEAD < steps)
        def _():
            fetch(i + AHEAD).start()

        repack(i, ones, held, made)
        store(i).start()
        return carry

    lax.fori_loop(0, steps, some, 0)
    for i in range(steps):
        store(i).wait()
    if offset > 0:
        state_copy.wait()


def margin_scratch(steps, step, flat, width):
    return [
        pltpu.VMEM((steps, step, flat), jnp.bfloat16),
        pltpu.VMEM((steps, step // 2, width, 2 * width), jnp.bfloat16),
        pltpu.SemaphoreType.DMA((steps,)),
        pltpu.SemaphoreType.DMA((steps,)),
    ]


def margin_tiles(margins, width):
    slots, partners, flat = margins.shape
    entries = slots * partners
    step = math.lcm(partners, ENTRIES)
    return pl.pallas_call(
        functools.partial(margin_kernel, 0),
        in_specs=[VMEM, HBM],
        out_specs=HBM,
        out_shape=jax.ShapeDtypeStruct((entries // 2, width, 2 * width), jnp.bfloat16),
        scratch_shapes=margin_scratch(FIRST, step, flat, width),
        cost_estimate=pl.CostEstimate(flops=0, bytes_accessed=4 * margins.size, transcendentals=0),
        compiler_params=pltpu.CompilerParams(vmem_limit_bytes=VMEM_LIMIT),
        name="margin_tiles",
    )(picker(), margins.reshape(entries, flat))


def more_tiles(tiles, margins, right_side, pno_energy, occ_energy, pno_count):
    slots, partners, flat = margins.shape
    width = pno_energy.shape[1]
    entries = slots * partners
    step = math.lcm(partners, ENTRIES)
    return pl.pallas_call(
        functools.partial(margin_kernel, FIRST),
        in_specs=[VMEM, HBM, HBM, SMEM, SMEM, VMEM, VMEM],
        out_specs=[HBM, HBM],
        out_shape=[
            jax.ShapeDtypeStruct(tiles.shape, tiles.dtype),
            jax.ShapeDtypeStruct((STATE_ROOM, slots // 2, width, 2 * width), jnp.float32),
        ],
        scratch_shapes=[
            *margin_scratch(entries // step - FIRST, step, flat, width),
            pltpu.VMEM((slots * width, 2 * width), jnp.float32),
            pltpu.VMEM((4, slots // 2, width, 2 * width), jnp.float32),
            pltpu.SemaphoreType.DMA,
        ],
        input_output_aliases={2: 0},
        cost_estimate=pl.CostEstimate(flops=0, bytes_accessed=4 * margins.size, transcendentals=0),
        compiler_params=pltpu.CompilerParams(vmem_limit_bytes=VMEM_LIMIT),
        name="more_tiles",
    )(picker(), margins.reshape(entries, flat), tiles, pno_count, occ_energy, right_side, pno_energy)


def flat_kernel(count, occ, current, right, energy, out_hbm, store, out, done):
    slots, width = energy.shape
    half, lanes = slots // 2, 2 * width
    for u in range(half):
        tile = current[u]
        store[0, u * width : (u + 1) * width] = tile
        store[1, u * width : (u + 1) * width] = swap_halves(tile)
    slot = lax.broadcasted_iota(jnp.int32, (slots, lanes), 0)
    lane = lax.broadcasted_iota(jnp.int32, (slots, lanes), 1)
    shift = jnp.zeros((slots, lanes), jnp.float32)
    most = jnp.zeros((slots, lanes), jnp.int32)
    for s in range(slots):
        shift = jnp.where(slot == s, occ[s], shift)
        most = jnp.where(slot == s, count[s], most)
    left = lane < width
    across = energy[...]
    along = jnp.concatenate([across, across], axis=1)
    inside = lane % width < most
    for j in range(width // 2):
        columns = slice(j * lanes, (j + 1) * lanes)
        first = jnp.broadcast_to(across[:, 2 * j : 2 * j + 1], (slots, lanes))
        second = jnp.broadcast_to(across[:, 2 * j + 1 : 2 * j + 2], (slots, lanes))
        row = 2 * j + jnp.where(left, 0, 1)
        out[0, :, columns] = right[:, columns]
        out[1, :, columns] = jnp.where(left, first, second) + along - shift - FREQUENCY
        out[2, :, columns] = jnp.where(inside & (row < most), 1.0, 0.0)
        upper, lower = (store[0, pl.ds(2 * j + i, half, stride=width), :] for i in range(2))
        upper_turned, lower_turned = (store[1, pl.ds(2 * j + i, half, stride=width), :] for i in range(2))
        out[3, :half, columns] = jnp.where(left[:half], upper, lower_turned)
        out[3, half:, columns] = jnp.where(left[:half], upper_turned, lower)
    copy = pltpu.make_async_copy(out, out_hbm.at[:4], done)
    copy.start()
    copy.wait()


def flat_state(current, right_side, pno_energy, occ_energy, pno_count):
    slots, flat = right_side.shape
    width = pno_energy.shape[1]
    return pl.pallas_call(
        flat_kernel,
        in_specs=[SMEM, SMEM, VMEM, VMEM, VMEM],
        out_specs=HBM,
        out_shape=jax.ShapeDtypeStruct((STATE_ROOM, slots, flat), jnp.float32),
        scratch_shapes=[
            pltpu.VMEM((2, slots // 2 * width, 2 * width), jnp.float32),
            pltpu.VMEM((4, slots, flat), jnp.float32),
            pltpu.SemaphoreType.DMA,
        ],
        cost_estimate=pl.CostEstimate(flops=0, bytes_accessed=32 * right_side.size, transcendentals=0),
        name="flat_state",
    )(pno_count, occ_energy, current, right_side, pno_energy)


def couple_kernel(last, pieces, place, partners, *refs):
    gathered, refs = refs[:pieces], refs[pieces:]
    margins, state, *outs = refs[:4]
    expanded, held, halves, coupled, steady, arrived = refs[4:10]
    slots, pairs, width, lanes = held.shape
    half = slots // 2

    def fetch(i):
        return pltpu.make_async_copy(margins.at[i], held.at[i], arrived.at[i])

    fetch_state = pltpu.make_async_copy(state.at[:4], steady, arrived.at[slots])
    for i in range(SLOTS_AT_ONCE):
        fetch(i).start()
    left = left_lanes(width)
    at = 0
    for piece in gathered:

        def expand(i, at, piece=piece):
            tile = piece[i]
            turned = swap_halves(tile)
            zero = jnp.zeros_like(tile)
            expanded[at] = jnp.where(left, tile, zero)
            expanded[at + 1] = jnp.where(left, zero, turned)
            expanded[at + 2] = jnp.where(left, turned, zero)
            expanded[at + 3] = jnp.where(left, zero, tile)
            return at + 4

        at = lax.fori_loop(0, piece.shape[0], expand, at, unroll=half)

    def one_slot(s, at):
        for k in range(pairs):
            first, second = place[partners[s, 2 * k]], place[partners[s, 2 * k + 1]] + 1
            weights = jnp.concatenate([expanded[first], expanded[second]], axis=0)
            product = jnp.dot(held[s, k], weights, preferred_element_type=jnp.float32)
            halves[at, :, k * lanes : (k + 1) * lanes] = product.astype(jnp.bfloat16)
        margin = jnp.concatenate([held[s, k] for k in range(pairs)], axis=1)
        coupled[pl.ds(s * width, width)] = lax.dot_general(halves[at], margin, NT, preferred_element_type=jnp.float32)

    for i in range(SLOTS_AT_ONCE, slots):
        fetch(i).start()
    fetch_state.start()

    def some_slots(i, carry):
        for at in range(SLOTS_AT_ONCE):
            fetch(i * SLOTS_AT_ONCE + at).wait()
        for at in range(SLOTS_AT_ONCE):
            one_slot(i * SLOTS_AT_ONCE + at, at)
        return carry

    lax.fori_loop(0, slots // SLOTS_AT_ONCE, some_slots, 0)

    fetch_state.wait()
    if not last:
        for u in range(half):
            v = u + half
            both = jnp.concatenate(
                [coupled[u * width : (u + 1) * width], coupled[v * width : (v + 1) * width]], axis=1
            )
            right, denom, mask, before = (steady[i, u] for i in range(4))
            after = before + mask * (right - denom * before - both) / denom
            outs[0][u] = after
            outs[1][u] = after.astype(jnp.bfloat16)
        return
    made, sent = refs[10:]
    columns = width // 2 // CUTS * lanes

    def send(i, cut):
        some = pl.ds(cut * columns, columns)
        return pltpu.make_async_copy(made.at[i, :, some], outs[i].at[:, some], sent.at[i, cut])

    for cut in range(CUTS):
        for j in range(cut * width // 2 // CUTS, (cut + 1) * width // 2 // CUTS):
            here = slice(j * lanes, (j + 1) * lanes)
            both = jnp.concatenate([coupled[pl.ds(2 * j + i, slots, stride=width), :] for i in range(2)], axis=1)
            right, denom, mask, before = (steady[i, :, here] for i in range(4))
            residual = mask * (right - denom * before - both)
            made[0, :, here] = before + residual / denom
            made[1, :, here] = residual
        for i in range(2):
            send(i, cut).start()
    for cut in range(CUTS):
        for i in range(2):
            send(i, cut).wait()


def couple(place, partners, gathered, margins, state, last):
    slots, pairs, width, lanes = margins.shape
    half = slots // 2
    devices = sum(piece.shape[0] for piece in gathered) // half
    packed = jax.ShapeDtypeStruct((half, width, lanes), jnp.float32)
    flat = jax.ShapeDtypeStruct((slots, width * width), jnp.float32)
    blocks = jax.ShapeDtypeStruct((half, width, lanes), jnp.bfloat16)
    scratch = [
        pltpu.VMEM((2 * devices * slots, width, lanes), jnp.bfloat16),
        pltpu.VMEM((slots, pairs, width, lanes), jnp.bfloat16),
        pltpu.VMEM((SLOTS_AT_ONCE, width, pairs * lanes), jnp.bfloat16),
        pltpu.VMEM((slots * width, width), jnp.float32),
        pltpu.VMEM((4, *state.shape[1:]), jnp.float32),
        pltpu.SemaphoreType.DMA((slots + 1,)),
    ]
    if last:
        scratch += [pltpu.VMEM((2, slots, width * width), jnp.float32), pltpu.SemaphoreType.DMA((2, CUTS))]
    return pl.pallas_call(
        functools.partial(couple_kernel, last, len(gathered)),
        in_specs=[SMEM] * 2 + [VMEM] * len(gathered) + [HBM] * 2,
        out_specs=[HBM] * 2 if last else [VMEM] * 2,
        out_shape=[flat, flat] if last else [packed, blocks],
        scratch_shapes=scratch,
        compiler_params=pltpu.CompilerParams(vmem_limit_bytes=COUPLE_LIMIT),
        name="couple",
    )(place, partners, *gathered, margins, state)


def gather(blocks, devices, first, second):
    work = first()
    if devices != 16:
        return [lax.all_gather(blocks, "pair", axis=0, tiled=True)], second(work)

    def swap(piece, other):
        return lax.ppermute(piece, "pair", [(i, i ^ other) for i in range(devices)])

    piece = {0: blocks}
    for other in (2, 4, 12):
        piece[other] = swap(blocks, other)
    piece[12], work = lax.optimization_barrier((piece[12], work))
    work = second(work)
    piece[8] = swap(piece[12], 4)
    piece[10] = swap(piece[12], 6)
    piece[14] = swap(piece[12], 2)
    piece[6] = swap(piece[4], 2)
    piece[10], work = lax.optimization_barrier((piece[10], work))
    for other in (0, 2, 4, 12, 6, 14, 8, 10):
        piece[other ^ 1] = swap(piece[other], 1)
    return [piece[i] for i in range(devices)], work


def shards(right_side, pno_energy, occ_energy, pno_count, margins, partners, slot_of):
    devices = lax.axis_size("pair")
    slots, entries = partners.shape
    width = pno_energy.shape[1]
    own = right_side, pno_energy, occ_energy, pno_count
    place = places(slot_of, slots, lax.axis_index("pair") if devices == 16 else 0)
    gathered, (tiles, state) = gather(
        start(*own), devices, lambda: margin_tiles(margins, width), lambda tiles: more_tiles(tiles, margins, *own)
    )
    tiles = tiles.reshape(slots, entries // 2, width, 2 * width)
    current, blocks = couple(place, partners, gathered, tiles, state, False)
    gathered, state = gather(blocks, devices, lambda: flat_state(current, *own), lambda state: state)
    return tuple(couple(place, partners, gathered, tiles, state, True))


def solution(mesh):
    placed = (
        P(("groups", "pair"), None),
        P(("groups", "pair"), None),
        P(("groups", "pair")),
        P(("groups", "pair")),
        P(("groups", "pair"), None, None),
        P(("groups", "pair"), None),
        P("groups"),
    )
    return jax.shard_map(
        shards,
        mesh=mesh,
        in_specs=placed,
        out_specs=(P(("groups", "pair"), None), P(("groups", "pair"), None)),
        check_vma=False,
    )
```

```python
import functools
import math

import jax
import jax.numpy as jnp
import numpy as np
from jax import lax
from jax.experimental import pallas as pl
from jax.experimental.pallas import tpu as pltpu
from jax.sharding import PartitionSpec as P

FREQUENCY = 0.25
BUFFERS = 8
ENTRIES = 16
TILES = 8
FIRST = 6
AHEAD = 8
CUTS = 2
NT = (((1,), (1,)), ((), ()))
VMEM = pl.BlockSpec(memory_space=pltpu.VMEM)
SMEM = pl.BlockSpec(memory_space=pltpu.SMEM)
VMEM_LIMIT = 58 * 2**20
STATE_ROOM = 16
FLAT_LIMIT = 8 * 2**20
COUPLE_LIMIT = 50 * 2**20
HBM = pl.BlockSpec(memory_space=pltpu.HBM)


def left_lanes(width):
    return lax.broadcasted_iota(jnp.int32, (width, 2 * width), 1) < width


def swap_halves(tile):
    width = tile.shape[1] // 2
    return jnp.concatenate([tile[:, width:], tile[:, :width]], axis=1)


def begin(count, occ, right, energy, rows):
    slots, width = energy.shape
    half = slots // 2
    lanes = 2 * width
    slot = lax.broadcasted_iota(jnp.int32, (slots, lanes), 0)
    for j in range(width // 2):
        part = right[:, j * lanes : (j + 1) * lanes]
        turned = swap_halves(part)
        rows[pl.ds(2 * j, slots, stride=width), :] = jnp.where(slot < half, part, turned)
        rows[pl.ds(2 * j + 1, slots, stride=width), :] = jnp.where(slot < half, turned, part)
    left = left_lanes(width)
    row = lax.broadcasted_iota(jnp.int32, (width, lanes), 0)
    column = lax.broadcasted_iota(jnp.int32, (width, lanes), 1) % width
    across = energy[...]
    down = across.T
    for u in range(half):
        v = u + half
        first = jnp.broadcast_to(down[:, u : u + 1], (width, lanes))
        second = jnp.broadcast_to(down[:, v : v + 1], (width, lanes))
        along = jnp.concatenate([across[u : u + 1], across[v : v + 1]], axis=1)
        shift = jnp.where(left, occ[u], occ[v])
        denom = jnp.where(left, first, second) + along - shift - FREQUENCY
        most = jnp.where(left, count[u], count[v])
        mask = jnp.where((row < most) & (column < most), 1.0, 0.0)
        yield u, jnp.where(left, rows[u * width : (u + 1) * width], rows[v * width : (v + 1) * width]), denom, mask


def start_kernel(count, occ, right, energy, blocks_out, rows):
    for u, tile, denom, mask in begin(count, occ, right, energy, rows):
        blocks_out[u] = (mask * tile / denom).astype(jnp.bfloat16)


def start(right_side, pno_energy, occ_energy, pno_count):
    slots, width = pno_energy.shape
    return pl.pallas_call(
        start_kernel,
        in_specs=[SMEM, SMEM, VMEM, VMEM],
        out_specs=VMEM,
        out_shape=jax.ShapeDtypeStruct((slots // 2, width, 2 * width), jnp.bfloat16),
        scratch_shapes=[pltpu.VMEM((slots * width, 2 * width), jnp.float32)],
        name="start",
    )(pno_count, occ_energy, right_side, pno_energy)


def places(slot_of, slots, twist):
    half = slots // 2
    device, slot = slot_of // slots, slot_of % slots
    return 4 * ((device ^ twist) * half + slot % half) + 2 * (slot // half)


def picker():
    pair, line = np.divmod(np.arange(ENTRIES * TILES), 2 * TILES)
    ones = np.zeros((ENTRIES * TILES, 2 * TILES * ENTRIES), np.float32)
    for side in range(2):
        ones[np.arange(ENTRIES * TILES), (line % 2) * TILES * ENTRIES + (line // 2) * ENTRIES + 2 * pair + side] = 1
    return jnp.asarray(ones, jnp.bfloat16)


def repack(i, ones, held, made):
    step, width, lanes = held.shape[1], *made.shape[2:]
    left = lax.broadcasted_iota(jnp.int32, (ENTRIES, lanes), 1) < width
    even = lax.broadcasted_iota(jnp.int32, (ENTRIES, lanes), 0) % 2 == 0
    for group in range(step // ENTRIES):
        rows = slice(group * ENTRIES, (group + 1) * ENTRIES)
        for n in range(0, width // 2, 2 * TILES):
            sides = []
            for part in (n, n + TILES):
                upper, lower = [], []
                for j in range(part, part + TILES):
                    here = held[i, rows, j * lanes : (j + 1) * lanes]
                    turned = swap_halves(here)
                    zero = jnp.zeros_like(here)
                    upper.append(jnp.where(left & even, here, jnp.where(left | even, zero, turned)))
                    lower.append(jnp.where(left & even, turned, jnp.where(left | even, zero, here)))
                sides.append(jnp.concatenate(upper + lower, axis=0))
            both = jnp.concatenate(sides, axis=1)
            found = jnp.dot(ones, both, preferred_element_type=jnp.float32).astype(jnp.bfloat16)
            for pair in range(ENTRIES // 2):
                for side in range(2):
                    line = 2 * (n + side * TILES)
                    made[i, group * (ENTRIES // 2) + pair, line : line + 2 * TILES] = found[
                        pair * 2 * TILES : (pair + 1) * 2 * TILES, side * lanes : (side + 1) * lanes
                    ]


def margin_kernel(offset, pick, margins, *refs):
    if offset > 0:
        _, count, occ, right, energy, tiles, state, *refs, rows, out, done = refs
        refs = tiles, *refs
    tiles, held, made, arrived, left_for = refs
    steps, step = held.shape[:2]

    def fetch(i):
        return pltpu.make_async_copy(margins.at[pl.ds((offset + i) * step, step)], held.at[i], arrived.at[i])

    def store(i):
        some = pl.ds((offset + i) * (step // 2), step // 2)
        return pltpu.make_async_copy(made.at[i], tiles.at[some], left_for.at[i])

    for i in range(min(AHEAD, steps)):
        fetch(i).start()
    if offset > 0:
        for u, tile, denom, mask in begin(count, occ, right, energy, rows):
            out[0, u] = tile
            out[1, u] = denom
            out[2, u] = mask
            out[3, u] = mask * tile / denom
        state_copy = pltpu.make_async_copy(out, state.at[:4], done)
        state_copy.start()
    ones = pick[...]

    def some(i, carry):
        fetch(i).wait()

        @pl.when(i + AHEAD < steps)
        def _():
            fetch(i + AHEAD).start()

        repack(i, ones, held, made)
        store(i).start()
        return carry

    lax.fori_loop(0, steps, some, 0)
    for i in range(steps):
        store(i).wait()
    if offset > 0:
        state_copy.wait()


def margin_scratch(steps, step, flat, width):
    return [
        pltpu.VMEM((steps, step, flat), jnp.bfloat16),
        pltpu.VMEM((steps, step // 2, width, 2 * width), jnp.bfloat16),
        pltpu.SemaphoreType.DMA((steps,)),
        pltpu.SemaphoreType.DMA((steps,)),
    ]


def margin_tiles(margins, width):
    slots, partners, flat = margins.shape
    entries = slots * partners
    step = math.lcm(partners, ENTRIES)
    return pl.pallas_call(
        functools.partial(margin_kernel, 0),
        in_specs=[VMEM, HBM],
        out_specs=HBM,
        out_shape=jax.ShapeDtypeStruct((entries // 2, width, 2 * width), jnp.bfloat16),
        scratch_shapes=margin_scratch(FIRST, step, flat, width),
        cost_estimate=pl.CostEstimate(flops=0, bytes_accessed=4 * margins.size, transcendentals=0),
        compiler_params=pltpu.CompilerParams(vmem_limit_bytes=VMEM_LIMIT),
        name="margin_tiles",
    )(picker(), margins.reshape(entries, flat))


def more_tiles(tiles, margins, right_side, pno_energy, occ_energy, pno_count):
    slots, partners, flat = margins.shape
    width = pno_energy.shape[1]
    entries = slots * partners
    step = math.lcm(partners, ENTRIES)
    return pl.pallas_call(
        functools.partial(margin_kernel, FIRST),
        in_specs=[VMEM, HBM, HBM, SMEM, SMEM, VMEM, VMEM],
        out_specs=[HBM, HBM],
        out_shape=[
            jax.ShapeDtypeStruct(tiles.shape, tiles.dtype),
            jax.ShapeDtypeStruct((STATE_ROOM, slots // 2, width, 2 * width), jnp.float32),
        ],
        scratch_shapes=[
            *margin_scratch(entries // step - FIRST, step, flat, width),
            pltpu.VMEM((slots * width, 2 * width), jnp.float32),
            pltpu.VMEM((4, slots // 2, width, 2 * width), jnp.float32),
            pltpu.SemaphoreType.DMA,
        ],
        input_output_aliases={2: 0},
        cost_estimate=pl.CostEstimate(flops=0, bytes_accessed=4 * margins.size, transcendentals=0),
        compiler_params=pltpu.CompilerParams(vmem_limit_bytes=VMEM_LIMIT),
        name="more_tiles",
    )(picker(), margins.reshape(entries, flat), tiles, pno_count, occ_energy, right_side, pno_energy)


def flat_kernel(count, occ, current, right, energy, out_hbm, store, out, done):
    slots, width = energy.shape
    half, lanes = slots // 2, 2 * width
    for u in range(half):
        tile = current[u]
        store[0, u * width : (u + 1) * width] = tile
        store[1, u * width : (u + 1) * width] = swap_halves(tile)
    slot = lax.broadcasted_iota(jnp.int32, (slots, lanes), 0)
    lane = lax.broadcasted_iota(jnp.int32, (slots, lanes), 1)
    shift = jnp.zeros((slots, lanes), jnp.float32)
    most = jnp.zeros((slots, lanes), jnp.int32)
    for s in range(slots):
        shift = jnp.where(slot == s, occ[s], shift)
        most = jnp.where(slot == s, count[s], most)
    left = lane < width
    across = energy[...]
    along = jnp.concatenate([across, across], axis=1)
    inside = lane % width < most
    for j in range(width // 2):
        columns = slice(j * lanes, (j + 1) * lanes)
        first = jnp.broadcast_to(across[:, 2 * j : 2 * j + 1], (slots, lanes))
        second = jnp.broadcast_to(across[:, 2 * j + 1 : 2 * j + 2], (slots, lanes))
        row = 2 * j + jnp.where(left, 0, 1)
        out[0, :, columns] = right[:, columns]
        out[1, :, columns] = jnp.where(left, first, second) + along - shift - FREQUENCY
        out[2, :, columns] = jnp.where(inside & (row < most), 1.0, 0.0)
        upper, lower = (store[0, pl.ds(2 * j + i, half, stride=width), :] for i in range(2))
        upper_turned, lower_turned = (store[1, pl.ds(2 * j + i, half, stride=width), :] for i in range(2))
        out[3, :half, columns] = jnp.where(left[:half], upper, lower_turned)
        out[3, half:, columns] = jnp.where(left[:half], upper_turned, lower)
    copy = pltpu.make_async_copy(out, out_hbm.at[:4], done)
    copy.start()
    copy.wait()


def flat_state(current, right_side, pno_energy, occ_energy, pno_count):
    slots, flat = right_side.shape
    width = pno_energy.shape[1]
    return pl.pallas_call(
        flat_kernel,
        in_specs=[SMEM, SMEM, VMEM, VMEM, VMEM],
        out_specs=HBM,
        out_shape=jax.ShapeDtypeStruct((STATE_ROOM, slots, flat), jnp.float32),
        scratch_shapes=[
            pltpu.VMEM((2, slots // 2 * width, 2 * width), jnp.float32),
            pltpu.VMEM((4, slots, flat), jnp.float32),
            pltpu.SemaphoreType.DMA,
        ],
        cost_estimate=pl.CostEstimate(flops=0, bytes_accessed=32 * right_side.size, transcendentals=0),
        compiler_params=pltpu.CompilerParams(vmem_limit_bytes=FLAT_LIMIT),
        name="flat_state",
    )(pno_count, occ_energy, current, right_side, pno_energy)


def couple_kernel(last, pieces, place, partners, *refs):
    gathered, refs = refs[:pieces], refs[pieces:]
    margins, state, *outs = refs[:4]
    expanded, held, halves, coupled, steady, arrived = refs[4:10]
    slots, pairs, width, lanes = held.shape
    half = slots // 2

    parts = ((0, slots // 4), (slots // 4, slots - slots // 4))

    def fetch(i):
        some = pl.ds(*parts[i])
        return pltpu.make_async_copy(margins.at[some], held.at[some], arrived.at[i])

    fetch_state = pltpu.make_async_copy(state.at[:4], steady, arrived.at[len(parts)])
    for i in range(len(parts)):
        fetch(i).start()
    fetch_state.start()
    left = left_lanes(width)
    at = 0
    for piece in gathered:

        def expand(i, at, piece=piece):
            tile = piece[i]
            turned = swap_halves(tile)
            zero = jnp.zeros_like(tile)
            expanded[at] = jnp.where(left, tile, zero)
            expanded[at + 1] = jnp.where(left, zero, turned)
            expanded[at + 2] = jnp.where(left, turned, zero)
            expanded[at + 3] = jnp.where(left, zero, tile)
            return at + 4

        at = lax.fori_loop(0, piece.shape[0], expand, at, unroll=half)

    def one_slot(s, at):
        for k in range(pairs):
            first, second = place[partners[s, 2 * k]], place[partners[s, 2 * k + 1]] + 1
            weights = jnp.concatenate([expanded[first], expanded[second]], axis=0)
            product = jnp.dot(held[s, k], weights, preferred_element_type=jnp.float32)
            halves[at, :, k * lanes : (k + 1) * lanes] = product.astype(jnp.bfloat16)
        margin = jnp.concatenate([held[s, k] for k in range(pairs)], axis=1)
        coupled[s * width : (s + 1) * width] = lax.dot_general(halves[at], margin, NT, preferred_element_type=jnp.float32)

    for i, (first, some) in enumerate(parts):
        fetch(i).wait()
        for s in range(first, first + some):
            one_slot(s, s % BUFFERS)

    fetch_state.wait()
    if not last:
        for u in range(half):
            v = u + half
            both = jnp.concatenate(
                [coupled[u * width : (u + 1) * width], coupled[v * width : (v + 1) * width]], axis=1
            )
            right, denom, mask, before = (steady[i, u] for i in range(4))
            after = before + mask * (right - denom * before - both) / denom
            outs[0][u] = after
            outs[1][u] = after.astype(jnp.bfloat16)
        return
    made, sent = refs[10:]
    columns = width // 2 // CUTS * lanes

    def send(i, cut):
        some = pl.ds(cut * columns, columns)
        return pltpu.make_async_copy(made.at[i, :, some], outs[i].at[:, some], sent.at[i, cut])

    for cut in range(CUTS):
        for j in range(cut * width // 2 // CUTS, (cut + 1) * width // 2 // CUTS):
            here = slice(j * lanes, (j + 1) * lanes)
            both = jnp.concatenate([coupled[pl.ds(2 * j + i, slots, stride=width), :] for i in range(2)], axis=1)
            right, denom, mask, before = (steady[i, :, here] for i in range(4))
            residual = mask * (right - denom * before - both)
            made[0, :, here] = before + residual / denom
            made[1, :, here] = residual
        for i in range(2):
            send(i, cut).start()
    for cut in range(CUTS):
        for i in range(2):
            send(i, cut).wait()


def couple(place, partners, gathered, margins, state, last):
    slots, pairs, width, lanes = margins.shape
    half = slots // 2
    devices = sum(piece.shape[0] for piece in gathered) // half
    packed = jax.ShapeDtypeStruct((half, width, lanes), jnp.float32)
    flat = jax.ShapeDtypeStruct((slots, width * width), jnp.float32)
    blocks = jax.ShapeDtypeStruct((half, width, lanes), jnp.bfloat16)
    scratch = [
        pltpu.VMEM((2 * devices * slots, width, lanes), jnp.bfloat16),
        pltpu.VMEM((slots, pairs, width, lanes), jnp.bfloat16),
        pltpu.VMEM((BUFFERS, width, pairs * lanes), jnp.bfloat16),
        pltpu.VMEM((slots * width, width), jnp.float32),
        pltpu.VMEM((4, *state.shape[1:]), jnp.float32),
        pltpu.SemaphoreType.DMA((3,)),
    ]
    if last:
        scratch += [pltpu.VMEM((2, slots, width * width), jnp.float32), pltpu.SemaphoreType.DMA((2, CUTS))]
    return pl.pallas_call(
        functools.partial(couple_kernel, last, len(gathered)),
        in_specs=[SMEM] * 2 + [VMEM] * len(gathered) + [HBM] * 2,
        out_specs=[HBM] * 2 if last else [VMEM] * 2,
        out_shape=[flat, flat] if last else [packed, blocks],
        scratch_shapes=scratch,
        compiler_params=pltpu.CompilerParams(vmem_limit_bytes=COUPLE_LIMIT),
        name="couple",
    )(place, partners, *gathered, margins, state)


def gather(blocks, devices, first, second):
    work = first()
    if devices != 16:
        return [lax.all_gather(blocks, "pair", axis=0, tiled=True)], second(work)

    def swap(piece, other):
        return lax.ppermute(piece, "pair", [(i, i ^ other) for i in range(devices)])

    piece = {0: blocks}
    for other in (2, 4, 12):
        piece[other] = swap(blocks, other)
    piece[12], work = lax.optimization_barrier((piece[12], work))
    work = second(work)
    piece[8] = swap(piece[12], 4)
    piece[10] = swap(piece[12], 6)
    piece[14] = swap(piece[12], 2)
    piece[6] = swap(piece[4], 2)
    piece[10], work = lax.optimization_barrier((piece[10], work))
    for other in (0, 2, 4, 12, 6, 14, 8, 10):
        piece[other ^ 1] = swap(piece[other], 1)
    return [piece[i] for i in range(devices)], work


def shards(right_side, pno_energy, occ_energy, pno_count, margins, partners, slot_of):
    devices = lax.axis_size("pair")
    slots, entries = partners.shape
    width = pno_energy.shape[1]
    own = right_side, pno_energy, occ_energy, pno_count
    place = places(slot_of, slots, lax.axis_index("pair") if devices == 16 else 0)
    gathered, (tiles, state) = gather(
        start(*own), devices, lambda: margin_tiles(margins, width), lambda tiles: more_tiles(tiles, margins, *own)
    )
    tiles = tiles.reshape(slots, entries // 2, width, 2 * width)
    current, blocks = couple(place, partners, gathered, tiles, state, False)
    gathered, state = gather(blocks, devices, lambda: flat_state(current, *own), lambda state: state)
    return tuple(couple(place, partners, gathered, tiles, state, True))


def solution(mesh):
    placed = (
        P(("groups", "pair"), None),
        P(("groups", "pair"), None),
        P(("groups", "pair")),
        P(("groups", "pair")),
        P(("groups", "pair"), None, None),
        P(("groups", "pair"), None),
        P("groups"),
    )
    return jax.shard_map(
        shards,
        mesh=mesh,
        in_specs=placed,
        out_specs=(P(("groups", "pair"), None), P(("groups", "pair"), None)),
        check_vma=False,
    )
```

```python
import functools
import math

import jax
import jax.numpy as jnp
import numpy as np
from jax import lax
from jax.experimental import pallas as pl
from jax.experimental.pallas import tpu as pltpu
from jax.sharding import PartitionSpec as P

FREQUENCY = 0.25
BUFFERS = 8
ENTRIES = 16
TILES = 8
FIRST = 6
AHEAD = 8
CUTS = 2
NT = (((1,), (1,)), ((), ()))
VMEM = pl.BlockSpec(memory_space=pltpu.VMEM)
SMEM = pl.BlockSpec(memory_space=pltpu.SMEM)
VMEM_LIMIT = 58 * 2**20
STATE_ROOM = 16
FLAT_LIMIT = 8 * 2**20
COUPLE_LIMIT = 50 * 2**20
HBM = pl.BlockSpec(memory_space=pltpu.HBM)


def left_lanes(width):
    return lax.broadcasted_iota(jnp.int32, (width, 2 * width), 1) < width


def swap_halves(tile):
    width = tile.shape[1] // 2
    return jnp.concatenate([tile[:, width:], tile[:, :width]], axis=1)


def begin(count, occ, right, energy, rows):
    slots, width = energy.shape
    half = slots // 2
    lanes = 2 * width
    slot = lax.broadcasted_iota(jnp.int32, (slots, lanes), 0)
    for j in range(width // 2):
        part = right[:, j * lanes : (j + 1) * lanes]
        turned = swap_halves(part)
        rows[pl.ds(2 * j, slots, stride=width), :] = jnp.where(slot < half, part, turned)
        rows[pl.ds(2 * j + 1, slots, stride=width), :] = jnp.where(slot < half, turned, part)
    left = left_lanes(width)
    row = lax.broadcasted_iota(jnp.int32, (width, lanes), 0)
    column = lax.broadcasted_iota(jnp.int32, (width, lanes), 1) % width
    across = energy[...]
    down = across.T
    for u in range(half):
        v = u + half
        first = jnp.broadcast_to(down[:, u : u + 1], (width, lanes))
        second = jnp.broadcast_to(down[:, v : v + 1], (width, lanes))
        along = jnp.concatenate([across[u : u + 1], across[v : v + 1]], axis=1)
        shift = jnp.where(left, occ[u], occ[v])
        denom = jnp.where(left, first, second) + along - shift - FREQUENCY
        most = jnp.where(left, count[u], count[v])
        mask = jnp.where((row < most) & (column < most), 1.0, 0.0)
        yield u, jnp.where(left, rows[u * width : (u + 1) * width], rows[v * width : (v + 1) * width]), denom, mask


def start_kernel(count, occ, right, energy, blocks_out, rows):
    for u, tile, denom, mask in begin(count, occ, right, energy, rows):
        blocks_out[u] = (mask * tile / denom).astype(jnp.bfloat16)


def start(right_side, pno_energy, occ_energy, pno_count):
    slots, width = pno_energy.shape
    return pl.pallas_call(
        start_kernel,
        in_specs=[SMEM, SMEM, VMEM, VMEM],
        out_specs=VMEM,
        out_shape=jax.ShapeDtypeStruct((slots // 2, width, 2 * width), jnp.bfloat16),
        scratch_shapes=[pltpu.VMEM((slots * width, 2 * width), jnp.float32)],
        name="start",
    )(pno_count, occ_energy, right_side, pno_energy)


def places(slot_of, slots, twist):
    half = slots // 2
    device, slot = slot_of // slots, slot_of % slots
    return 4 * ((device ^ twist) * half + slot % half) + 2 * (slot // half)


def picker():
    pair, line = np.divmod(np.arange(ENTRIES * TILES), 2 * TILES)
    ones = np.zeros((ENTRIES * TILES, 2 * TILES * ENTRIES), np.float32)
    for side in range(2):
        ones[np.arange(ENTRIES * TILES), (line % 2) * TILES * ENTRIES + (line // 2) * ENTRIES + 2 * pair + side] = 1
    return jnp.asarray(ones, jnp.bfloat16)


def repack(i, ones, held, made):
    step, width, lanes = held.shape[1], *made.shape[2:]
    left = lax.broadcasted_iota(jnp.int32, (ENTRIES, lanes), 1) < width
    even = lax.broadcasted_iota(jnp.int32, (ENTRIES, lanes), 0) % 2 == 0
    for group in range(step // ENTRIES):
        rows = slice(group * ENTRIES, (group + 1) * ENTRIES)
        for n in range(0, width // 2, 2 * TILES):
            sides = []
            for part in (n, n + TILES):
                upper, lower = [], []
                for j in range(part, part + TILES):
                    here = held[i, rows, j * lanes : (j + 1) * lanes]
                    turned = swap_halves(here)
                    zero = jnp.zeros_like(here)
                    upper.append(jnp.where(left & even, here, jnp.where(left | even, zero, turned)))
                    lower.append(jnp.where(left & even, turned, jnp.where(left | even, zero, here)))
                sides.append(jnp.concatenate(upper + lower, axis=0))
            both = jnp.concatenate(sides, axis=1)
            found = jnp.dot(ones, both, preferred_element_type=jnp.float32).astype(jnp.bfloat16)
            for pair in range(ENTRIES // 2):
                for side in range(2):
                    line = 2 * (n + side * TILES)
                    made[i, group * (ENTRIES // 2) + pair, line : line + 2 * TILES] = found[
                        pair * 2 * TILES : (pair + 1) * 2 * TILES, side * lanes : (side + 1) * lanes
                    ]


def margin_kernel(offset, pick, margins, *refs):
    if offset > 0:
        _, count, occ, right, energy, tiles, state, *refs, rows, out, done = refs
        refs = tiles, *refs
    tiles, held, made, arrived, left_for = refs
    steps, step = held.shape[:2]

    def fetch(i):
        return pltpu.make_async_copy(margins.at[pl.ds((offset + i) * step, step)], held.at[i], arrived.at[i])

    def store(i):
        some = pl.ds((offset + i) * (step // 2), step // 2)
        return pltpu.make_async_copy(made.at[i], tiles.at[some], left_for.at[i])

    for i in range(min(AHEAD, steps)):
        fetch(i).start()
    if offset > 0:
        for u, tile, denom, mask in begin(count, occ, right, energy, rows):
            out[0, u] = tile
            out[1, u] = denom
            out[2, u] = mask
            out[3, u] = mask * tile / denom
        state_copy = pltpu.make_async_copy(out, state.at[:4], done)
        state_copy.start()
    ones = pick[...]

    def some(i, carry):
        fetch(i).wait()

        @pl.when(i + AHEAD < steps)
        def _():
            fetch(i + AHEAD).start()

        repack(i, ones, held, made)
        store(i).start()
        return carry

    lax.fori_loop(0, steps, some, 0)
    for i in range(steps):
        store(i).wait()
    if offset > 0:
        state_copy.wait()


def margin_scratch(steps, step, flat, width):
    return [
        pltpu.VMEM((steps, step, flat), jnp.bfloat16),
        pltpu.VMEM((steps, step // 2, width, 2 * width), jnp.bfloat16),
        pltpu.SemaphoreType.DMA((steps,)),
        pltpu.SemaphoreType.DMA((steps,)),
    ]


def margin_tiles(margins, width):
    slots, partners, flat = margins.shape
    entries = slots * partners
    step = math.lcm(partners, ENTRIES)
    return pl.pallas_call(
        functools.partial(margin_kernel, 0),
        in_specs=[VMEM, HBM],
        out_specs=HBM,
        out_shape=jax.ShapeDtypeStruct((entries // 2, width, 2 * width), jnp.bfloat16),
        scratch_shapes=margin_scratch(FIRST, step, flat, width),
        cost_estimate=pl.CostEstimate(flops=0, bytes_accessed=4 * margins.size, transcendentals=0),
        compiler_params=pltpu.CompilerParams(vmem_limit_bytes=VMEM_LIMIT),
        name="margin_tiles",
    )(picker(), margins.reshape(entries, flat))


def more_tiles(tiles, margins, right_side, pno_energy, occ_energy, pno_count):
    slots, partners, flat = margins.shape
    width = pno_energy.shape[1]
    entries = slots * partners
    step = math.lcm(partners, ENTRIES)
    return pl.pallas_call(
        functools.partial(margin_kernel, FIRST),
        in_specs=[VMEM, HBM, HBM, SMEM, SMEM, VMEM, VMEM],
        out_specs=[HBM, HBM],
        out_shape=[
            jax.ShapeDtypeStruct(tiles.shape, tiles.dtype),
            jax.ShapeDtypeStruct((STATE_ROOM, slots // 2, width, 2 * width), jnp.float32),
        ],
        scratch_shapes=[
            *margin_scratch(entries // step - FIRST, step, flat, width),
            pltpu.VMEM((slots * width, 2 * width), jnp.float32),
            pltpu.VMEM((4, slots // 2, width, 2 * width), jnp.float32),
            pltpu.SemaphoreType.DMA,
        ],
        input_output_aliases={2: 0},
        cost_estimate=pl.CostEstimate(flops=0, bytes_accessed=4 * margins.size, transcendentals=0),
        compiler_params=pltpu.CompilerParams(vmem_limit_bytes=VMEM_LIMIT),
        name="more_tiles",
    )(picker(), margins.reshape(entries, flat), tiles, pno_count, occ_energy, right_side, pno_energy)


def flat_kernel(count, occ, current, right, energy, out_hbm, store, out, done):
    slots, width = energy.shape
    half, lanes = slots // 2, 2 * width
    for u in range(half):
        tile = current[u]
        store[0, u * width : (u + 1) * width] = tile
        store[1, u * width : (u + 1) * width] = swap_halves(tile)
    slot = lax.broadcasted_iota(jnp.int32, (slots, lanes), 0)
    lane = lax.broadcasted_iota(jnp.int32, (slots, lanes), 1)
    shift = jnp.zeros((slots, lanes), jnp.float32)
    most = jnp.zeros((slots, lanes), jnp.int32)
    for s in range(slots):
        shift = jnp.where(slot == s, occ[s], shift)
        most = jnp.where(slot == s, count[s], most)
    left = lane < width
    across = energy[...]
    along = jnp.concatenate([across, across], axis=1)
    inside = lane % width < most
    for j in range(width // 2):
        columns = slice(j * lanes, (j + 1) * lanes)
        first = jnp.broadcast_to(across[:, 2 * j : 2 * j + 1], (slots, lanes))
        second = jnp.broadcast_to(across[:, 2 * j + 1 : 2 * j + 2], (slots, lanes))
        row = 2 * j + jnp.where(left, 0, 1)
        out[0, :, columns] = right[:, columns]
        out[1, :, columns] = jnp.where(left, first, second) + along - shift - FREQUENCY
        out[2, :, columns] = jnp.where(inside & (row < most), 1.0, 0.0)
        upper, lower = (store[0, pl.ds(2 * j + i, half, stride=width), :] for i in range(2))
        upper_turned, lower_turned = (store[1, pl.ds(2 * j + i, half, stride=width), :] for i in range(2))
        out[3, :half, columns] = jnp.where(left[:half], upper, lower_turned)
        out[3, half:, columns] = jnp.where(left[:half], upper_turned, lower)
    copy = pltpu.make_async_copy(out, out_hbm.at[:4], done)
    copy.start()
    copy.wait()


def flat_state(current, right_side, pno_energy, occ_energy, pno_count):
    slots, flat = right_side.shape
    width = pno_energy.shape[1]
    return pl.pallas_call(
        flat_kernel,
        in_specs=[SMEM, SMEM, VMEM, VMEM, VMEM],
        out_specs=HBM,
        out_shape=jax.ShapeDtypeStruct((STATE_ROOM, slots, flat), jnp.float32),
        scratch_shapes=[
            pltpu.VMEM((2, slots // 2 * width, 2 * width), jnp.float32),
            pltpu.VMEM((4, slots, flat), jnp.float32),
            pltpu.SemaphoreType.DMA,
        ],
        cost_estimate=pl.CostEstimate(flops=0, bytes_accessed=32 * right_side.size, transcendentals=0),
        compiler_params=pltpu.CompilerParams(vmem_limit_bytes=FLAT_LIMIT),
        name="flat_state",
    )(pno_count, occ_energy, current, right_side, pno_energy)


def couple_kernel(last, pieces, place, partners, *refs):
    gathered, refs = refs[:pieces], refs[pieces:]
    margins, state, *outs = refs[:4]
    expanded, held, halves, coupled, steady, arrived = refs[4:10]
    slots, pairs, width, lanes = held.shape
    half = slots // 2

    parts = ((0, slots // 4), (slots // 4, slots - slots // 4))

    def fetch(i):
        some = pl.ds(*parts[i])
        return pltpu.make_async_copy(margins.at[some], held.at[some], arrived.at[i])

    fetch_state = pltpu.make_async_copy(state.at[:4], steady, arrived.at[len(parts)])
    for i in range(len(parts)):
        fetch(i).start()
    left = left_lanes(width)
    at = 0
    for piece in gathered:

        def expand(i, at, piece=piece):
            tile = piece[i]
            turned = swap_halves(tile)
            zero = jnp.zeros_like(tile)
            expanded[at] = jnp.where(left, tile, zero)
            expanded[at + 1] = jnp.where(left, zero, turned)
            expanded[at + 2] = jnp.where(left, turned, zero)
            expanded[at + 3] = jnp.where(left, zero, tile)
            return at + 4

        at = lax.fori_loop(0, piece.shape[0], expand, at, unroll=half)

    def one_slot(s, at):
        for k in range(pairs):
            first, second = place[partners[s, 2 * k]], place[partners[s, 2 * k + 1]] + 1
            weights = jnp.concatenate([expanded[first], expanded[second]], axis=0)
            product = jnp.dot(held[s, k], weights, preferred_element_type=jnp.float32)
            halves[at, :, k * lanes : (k + 1) * lanes] = product.astype(jnp.bfloat16)
        margin = jnp.concatenate([held[s, k] for k in range(pairs)], axis=1)
        coupled[s * width : (s + 1) * width] = lax.dot_general(halves[at], margin, NT, preferred_element_type=jnp.float32)

    for i, (first, some) in enumerate(parts):
        fetch(i).wait()
        if i == 0:
            fetch_state.start()
        for s in range(first, first + some):
            one_slot(s, s % BUFFERS)

    fetch_state.wait()
    if not last:
        for u in range(half):
            v = u + half
            both = jnp.concatenate(
                [coupled[u * width : (u + 1) * width], coupled[v * width : (v + 1) * width]], axis=1
            )
            right, denom, mask, before = (steady[i, u] for i in range(4))
            after = before + mask * (right - denom * before - both) / denom
            outs[0][u] = after
            outs[1][u] = after.astype(jnp.bfloat16)
        return
    made, sent = refs[10:]
    columns = width // 2 // CUTS * lanes

    def send(i, cut):
        some = pl.ds(cut * columns, columns)
        return pltpu.make_async_copy(made.at[i, :, some], outs[i].at[:, some], sent.at[i, cut])

    for cut in range(CUTS):
        for j in range(cut * width // 2 // CUTS, (cut + 1) * width // 2 // CUTS):
            here = slice(j * lanes, (j + 1) * lanes)
            both = jnp.concatenate([coupled[pl.ds(2 * j + i, slots, stride=width), :] for i in range(2)], axis=1)
            right, denom, mask, before = (steady[i, :, here] for i in range(4))
            residual = mask * (right - denom * before - both)
            made[0, :, here] = before + residual / denom
            made[1, :, here] = residual
        for i in range(2):
            send(i, cut).start()
    for cut in range(CUTS):
        for i in range(2):
            send(i, cut).wait()


def couple(place, partners, gathered, margins, state, last):
    slots, pairs, width, lanes = margins.shape
    half = slots // 2
    devices = sum(piece.shape[0] for piece in gathered) // half
    packed = jax.ShapeDtypeStruct((half, width, lanes), jnp.float32)
    flat = jax.ShapeDtypeStruct((slots, width * width), jnp.float32)
    blocks = jax.ShapeDtypeStruct((half, width, lanes), jnp.bfloat16)
    scratch = [
        pltpu.VMEM((2 * devices * slots, width, lanes), jnp.bfloat16),
        pltpu.VMEM((slots, pairs, width, lanes), jnp.bfloat16),
        pltpu.VMEM((BUFFERS, width, pairs * lanes), jnp.bfloat16),
        pltpu.VMEM((slots * width, width), jnp.float32),
        pltpu.VMEM((4, *state.shape[1:]), jnp.float32),
        pltpu.SemaphoreType.DMA((3,)),
    ]
    if last:
        scratch += [pltpu.VMEM((2, slots, width * width), jnp.float32), pltpu.SemaphoreType.DMA((2, CUTS))]
    return pl.pallas_call(
        functools.partial(couple_kernel, last, len(gathered)),
        in_specs=[SMEM] * 2 + [VMEM] * len(gathered) + [HBM] * 2,
        out_specs=[HBM] * 2 if last else [VMEM] * 2,
        out_shape=[flat, flat] if last else [packed, blocks],
        scratch_shapes=scratch,
        compiler_params=pltpu.CompilerParams(vmem_limit_bytes=COUPLE_LIMIT),
        name="couple",
    )(place, partners, *gathered, margins, state)


def gather(blocks, devices, first, second):
    work = first()
    if devices != 16:
        return [lax.all_gather(blocks, "pair", axis=0, tiled=True)], second(work)

    def swap(piece, other):
        return lax.ppermute(piece, "pair", [(i, i ^ other) for i in range(devices)])

    piece = {0: blocks}
    for other in (2, 4, 12):
        piece[other] = swap(blocks, other)
    piece[12], work = lax.optimization_barrier((piece[12], work))
    work = second(work)
    piece[8] = swap(piece[12], 4)
    piece[10] = swap(piece[12], 6)
    piece[14] = swap(piece[12], 2)
    piece[6] = swap(piece[4], 2)
    piece[10], work = lax.optimization_barrier((piece[10], work))
    for other in (0, 2, 4, 12, 6, 14, 8, 10):
        piece[other ^ 1] = swap(piece[other], 1)
    return [piece[i] for i in range(devices)], work


def shards(right_side, pno_energy, occ_energy, pno_count, margins, partners, slot_of):
    devices = lax.axis_size("pair")
    slots, entries = partners.shape
    width = pno_energy.shape[1]
    own = right_side, pno_energy, occ_energy, pno_count
    place = places(slot_of, slots, lax.axis_index("pair") if devices == 16 else 0)
    gathered, (tiles, state) = gather(
        start(*own), devices, lambda: margin_tiles(margins, width), lambda tiles: more_tiles(tiles, margins, *own)
    )
    tiles = tiles.reshape(slots, entries // 2, width, 2 * width)
    current, blocks = couple(place, partners, gathered, tiles, state, False)
    gathered, state = gather(blocks, devices, lambda: flat_state(current, *own), lambda state: state)
    return tuple(couple(place, partners, gathered, tiles, state, True))


def solution(mesh):
    placed = (
        P(("groups", "pair"), None),
        P(("groups", "pair"), None),
        P(("groups", "pair")),
        P(("groups", "pair")),
        P(("groups", "pair"), None, None),
        P(("groups", "pair"), None),
        P("groups"),
    )
    return jax.shard_map(
        shards,
        mesh=mesh,
        in_specs=placed,
        out_specs=(P(("groups", "pair"), None), P(("groups", "pair"), None)),
        check_vma=False,
    )
```
